256 devices in a mesh: seq: 16 (over y, z_hi, core), head: 16 (over x, z_lo).
Axes of the slice: x: 4, y: 4, z: 8 (z_hi: 2, z_lo: 4; z = z_hi * 4 + z_lo), core: 2. Of those that a mesh axis runs over, the one named last changes fastest.
Arguments:
- gen_ids: int32 [16, 16], replicated, may hold values from 0 to 8191
- embed_rows: bfloat16 [8192, 8192], P('head', 'seq'), may hold values from -6 to 6
- w_query: bfloat16 [8192, 8192], P('seq', 'head'), may hold values from -0.0625 to 0.0625
- w_key: bfloat16 [8192, 8192], P('seq', 'head'), may hold values from -0.0625 to 0.0625
- w_value: bfloat16 [8192, 8192], P('seq', 'head'), may hold values from -0.0625 to 0.0625
- w_out: bfloat16 [8192, 8192], P('head', 'seq'), may hold values from -0.0625 to 0.0625
- prompt_keys: bfloat16 [8192, 8192], P('seq', 'head'), may hold values from -420 to 420
- prompt_values: bfloat16 [8192, 8192], P('seq', 'head'), may hold values from -6 to 6
Outputs:
- attn_out: bfloat16 [256, 8192], P('seq', 'head')
The draws below stay inside these ranges and needn't reach their ends.
All inputs are finite; a program needn't handle non-finite values.
Results may differ from the reference program's by a relative error of at most 0.034.
Values may be sent and summed in bfloat16 or wider, within the bound.
A program may use at most 128 MiB of HBM per device.

```python
import math
import jax
import jax.numpy as jnp
from jax import lax

D = 8192
H = 64
HD = 128
VOCAB = 8192
S = 16
C = 16
P_SIZE = 8192


def draw_prompt_keys(key, part):
    key = jax.random.fold_in(key, 7)
    base_key = jax.random.fold_in(key, 0)
    entries = jax.random.normal(base_key, (P_SIZE, H * HD), jnp.float32)
    return entries.astype(jnp.bfloat16)


def with_ends(values, stream_key, low, high):
    index_at = [jax.random.randint(jax.random.fold_in(stream_key, axis), (), 0, length) for axis, length in enumerate(values.shape)]
    longest = values.shape.index(max(values.shape))
    neighbour = index_at[:longest] + [(index_at[longest] + 1) % values.shape[longest]] + index_at[longest + 1:]
    return values.at[tuple(index_at)].set(low).at[tuple(neighbour)].set(high)


def level_of(stream_key, extent, cuts, least, high):
    factor_of, own = 1.0, jax.random.fold_in(stream_key, 6)
    for position, parts in cuts:
        heights = jnp.exp(jax.random.uniform(jax.random.fold_in(own, position), (parts,), jnp.float32, least / len(cuts), high / len(cuts)))
        factor_of = factor_of * jnp.repeat(heights, extent[position] // parts).reshape([-1 if axis == position else 1 for axis in range(len(extent))])
    return factor_of


def bell_draw(key, extent, deviation, reach, cuts=(), held_as=jnp.bfloat16):
    result = deviation * jax.random.normal(key, extent, jnp.float32)
    if cuts:
        result = result * level_of(key, extent, cuts, -0.22, 0.18)
    return jnp.clip(result, -reach, reach).astype(held_as)


def setup_inputs(seed: int = 0) -> dict:
    key_of = jax.random.split(jax.random.key(seed), 9)
    gen_ids = with_ends(jax.random.randint(key_of[0], (C, S), 0, VOCAB), jax.random.fold_in(key_of[0], 1), 0, VOCAB - 1).astype(jnp.int32)
    embed_rows = bell_draw(key_of[1], (VOCAB, D), 1.0, 6.0, ((0, 16), (1, 16)))
    w_query = bell_draw(key_of[2], (D, H * HD), D ** -0.5, 0.0625, ((0, 16), (1, 16)))
    w_key = bell_draw(key_of[3], (D, H * HD), D ** -0.5, 0.0625, ((0, 16), (1, 16)))
    w_value = bell_draw(key_of[4], (D, H * HD), D ** -0.5, 0.0625, ((0, 16), (1, 16)))
    w_out = bell_draw(key_of[5], (H * HD, D), (H * HD) ** -0.5, 0.0625, ((0, 16), (1, 16)))
    prompt_keys = draw_prompt_keys(jax.random.fold_in(key_of[8], 71), 0)
    prompt_values = bell_draw(key_of[7], (P_SIZE, H * HD), 1.0, 6.0, ((0, 16), (1, 16)))
    return dict(gen_ids=gen_ids, embed_rows=embed_rows, w_query=w_query, w_key=w_key, w_value=w_value, w_out=w_out, prompt_keys=prompt_keys, prompt_values=prompt_values)


def rotate(vectors, positions):
    half_size = vectors.shape[-1] // 2
    frequency = 10000.0 ** (-jnp.arange(half_size, dtype=jnp.float32) / half_size)
    angles = positions.astype(jnp.float32)[:, None] * frequency[None, :]
    cosine = jnp.cos(angles)[:, None, :]
    sine_part = jnp.sin(angles)[:, None, :]
    former = vectors[..., :half_size]
    latter = vectors[..., half_size:]
    return jnp.concatenate([former * cosine - latter * sine_part, former * sine_part + latter * cosine], axis=-1)

def reference(gen_ids, embed_rows, w_query, w_key, w_value, w_out, prompt_keys, prompt_values):
    cand_count, step_count = gen_ids.shape
    prompt_rows = prompt_keys.shape[0]
    embedded = embed_rows[gen_ids.reshape(-1)]
    positions = prompt_rows + jnp.arange(step_count, dtype=jnp.int32)

    def project(weight):
        return jnp.dot(embedded, weight, preferred_element_type=jnp.float32).reshape(cand_count, step_count, H, HD)
    queries = rotate(project(w_query), positions).astype(jnp.bfloat16)
    gen_keys = rotate(project(w_key), positions).astype(jnp.bfloat16)
    gen_values = project(w_value).astype(jnp.bfloat16)
    score_scale = 1.0 / math.sqrt(HD)
    causal = jnp.arange(step_count)[None, :] <= jnp.arange(step_count)[:, None]

    def one_head(packed):
        head_query, head_key, head_value, prompt_key, prompt_value = packed
        query_float = head_query.astype(jnp.float32)
        prompt_scores = jnp.einsum('csd,pd->csp', query_float, prompt_key.astype(jnp.float32)) * score_scale
        own_scores = jnp.einsum('csd,ctd->cst', query_float, head_key.astype(jnp.float32)) * score_scale
        own_scores = jnp.where(causal[None], own_scores, -jnp.inf)
        peak = jnp.maximum(lax.optimization_barrier(jnp.max(prompt_scores, axis=-1)), lax.optimization_barrier(jnp.max(own_scores, axis=-1)))
        prompt_weights = jnp.exp(prompt_scores - peak[..., None])
        own_weights = jnp.exp(own_scores - peak[..., None])
        weight_sum = lax.optimization_barrier(jnp.sum(prompt_weights, axis=-1)) + lax.optimization_barrier(jnp.sum(own_weights, axis=-1))
        prompt_rounded = lax.optimization_barrier(prompt_weights.astype(jnp.bfloat16)).astype(jnp.float32)
        own_rounded = lax.optimization_barrier(own_weights.astype(jnp.bfloat16)).astype(jnp.float32)
        accumulated = jnp.einsum('csp,pd->csd', prompt_rounded, prompt_value.astype(jnp.float32))
        accumulated = accumulated + jnp.einsum('cst,ctd->csd', own_rounded, head_value.astype(jnp.float32))
        return (accumulated / weight_sum[..., None]).astype(jnp.bfloat16)
    stacked_keys = prompt_keys.reshape(prompt_rows, H, HD).transpose(1, 0, 2)
    stacked_values = prompt_values.reshape(prompt_rows, H, HD).transpose(1, 0, 2)
    per_head = lax.map(one_head, (queries.transpose(2, 0, 1, 3), gen_keys.transpose(2, 0, 1, 3), gen_values.transpose(2, 0, 1, 3), stacked_keys, stacked_values))
    attended = per_head.transpose(1, 2, 0, 3).reshape(cand_count * step_count, H * HD)
    return jnp.dot(attended, w_out, preferred_element_type=jnp.float32).astype(jnp.bfloat16)
```

```python
import math

import jax
import jax.numpy as jnp
import numpy as np
from jax import lax
from jax.experimental import pallas as pl
from jax.experimental.pallas import tpu as pltpu
from jax.sharding import PartitionSpec as P

MESH = pl.DeviceIdType.MESH
HD = 128
N = 16
B = 16
F = 512
HEADS = F // HD
ST = 128
EXP_SCALE = math.log2(math.e) / math.sqrt(HD)
f32 = jnp.float32
bf16 = jnp.bfloat16


def rows_of(block):
    return pl.ds(pl.multiple_of(block * B, B), B)


def rounded(x):
    return x.astype(bf16).astype(f32)


def slot_sum(ref, columns=slice(None)):
    part = ref[:, columns].astype(f32)
    return jnp.sum(part.reshape(N, B, part.shape[-1]), axis=0)


def turned(x, table):
    heads = []
    for j in range(HEADS):
        part = x[:, j * HD : (j + 1) * HD]
        heads.append(part * table[:B] + pltpu.roll(part, HD // 2, 1) * table[B:])
    return jnp.concatenate(heads, axis=1)


def kernel(
    ids_hbm, e_hbm, wq_hbm, wk_hbm, wv_hbm, wo_hbm, k_hbm, v_hbm, tab_hbm, out_ref,
    ids, emb, wq, wk, wv, wo, keys, values, tab,
    pick, r_emb, x_all, q_part, r_q, q_all, kv_part, r_kv, o_part, r_o, att, out_part, r_out,
    load_sem, send_sem, recv_sem,
):
    s = lax.axis_index("seq")
    h = lax.axis_index("head")

    loads = [
        pltpu.make_async_copy(src, dst, load_sem.at[i])
        for i, (src, dst) in enumerate(
            [(ids_hbm, ids), (e_hbm, emb), (tab_hbm, tab), (wq_hbm, wq), (wk_hbm, wk), (wv_hbm, wv),
             (k_hbm, keys), (v_hbm, values), (wo_hbm, wo)]
        )
    ]
    for load in loads:
        load.start()

    barrier = pltpu.get_barrier_semaphore()

    def greet(d, carry):
        pl.semaphore_signal(barrier, inc=1, device_id=(s, lax.rem(h + d, N)), device_id_type=MESH)
        pl.semaphore_signal(barrier, inc=1, device_id=(lax.rem(s + d, N), h), device_id_type=MESH)
        return carry

    lax.fori_loop(1, N, greet, 0)

    def along_head(j):
        return (s, j)

    def along_seq(j):
        return (j, h)

    def scatter(i, src, dst, me, place):
        def step(d, carry):
            j = lax.rem(me + d, N)
            pltpu.make_async_remote_copy(
                src_ref=src.at[rows_of(j)], dst_ref=dst.at[rows_of(me)],
                send_sem=send_sem.at[i], recv_sem=recv_sem.at[i],
                device_id=place(j), device_id_type=MESH,
            ).start()
            return carry

        lax.fori_loop(1, N, step, 0)
        dst[rows_of(me), :] = src[rows_of(me), :]

    def spread(i, ref, me, place):
        def step(d, carry):
            pltpu.make_async_remote_copy(
                src_ref=ref.at[rows_of(me)], dst_ref=ref.at[rows_of(me)],
                send_sem=send_sem.at[i], recv_sem=recv_sem.at[i],
                device_id=place(lax.rem(me + d, N)), device_id_type=MESH,
            ).start()
            return carry

        lax.fori_loop(1, N, step, 0)

    def all_of(i, ref, place, count=N - 1):
        part = ref.at[pl.ds(0, count * B)]
        return pltpu.make_async_remote_copy(
            src_ref=part, dst_ref=part, send_sem=send_sem.at[i], recv_sem=recv_sem.at[i],
            device_id=place, device_id_type=MESH,
        )

    head_peer = (s, lax.rem(h + 1, N))
    seq_peer = (lax.rem(s + 1, N), h)

    loads[0].wait()
    shifted = (ids[...] - h * F).astype(f32)
    eye = lax.broadcasted_iota(jnp.int32, (B, B), 0) == lax.broadcasted_iota(jnp.int32, (B, B), 1)
    entry = lax.broadcasted_iota(jnp.int32, (B, F), 1).astype(f32)
    chosen = []
    for c in range(N):
        row = jnp.broadcast_to(shifted[c : c + 1, :], (B, B))
        column = jnp.sum(jnp.where(eye, row, 0.0), axis=1, keepdims=True)
        chosen.append(jnp.where(column == entry, 1.0, 0.0).astype(bf16))
    selector = jnp.concatenate(chosen, axis=0)
    loads[1].wait()
    pick[...] = jnp.dot(selector, emb[...], preferred_element_type=f32).astype(bf16)

    pl.semaphore_wait(barrier, 2 * (N - 1))

    scatter(0, pick, r_emb, h, along_head)
    all_of(0, r_emb, head_peer).wait_recv()
    x_all[rows_of(h), :] = slot_sum(r_emb).astype(bf16)
    spread(1, x_all, h, along_head)
    loads[3].wait()
    all_of(1, x_all, head_peer).wait_recv()

    q_part[...] = jnp.dot(x_all[...], wq[...], preferred_element_type=f32).astype(bf16)
    scatter(2, q_part, r_q, s, along_seq)
    loads[4].wait()
    loads[5].wait()
    kv_part[:, :F] = jnp.dot(x_all[...], wk[...], preferred_element_type=f32).astype(bf16)
    kv_part[:, F:] = jnp.dot(x_all[...], wv[...], preferred_element_type=f32).astype(bf16)
    loads[2].wait()
    table = tab[...]
    all_of(2, r_q, seq_peer).wait_recv()
    queries = turned(slot_sum(r_q), table).astype(bf16)
    q_all[rows_of(s), :] = queries
    spread(3, q_all, s, along_seq)
    scatter(4, kv_part, r_kv, s, along_seq)
    loads[6].wait()
    loads[7].wait()
    all_of(3, q_all, seq_peer).wait_recv()

    lane = lax.broadcasted_iota(jnp.int32, (N * B, ST), 1)
    peaks = jnp.zeros((N * B, ST), f32)
    sums = jnp.zeros((N * B, ST), f32)
    for j in range(HEADS):
        cols = slice(j * HD, (j + 1) * HD)
        scores = lax.dot_general(
            q_all[:, cols], keys[:, cols], (((1,), (1,)), ((), ())), preferred_element_type=f32
        )
        peak = jnp.max(scores, axis=1, keepdims=True)
        weights = jnp.exp2((scores - peak) * EXP_SCALE)
        total = jnp.sum(weights, axis=1, keepdims=True)
        o_part[:, cols] = jnp.dot(
            weights.astype(bf16), values[:, cols], preferred_element_type=f32
        ).astype(bf16)
        peaks = jnp.where(lane == j, peak, peaks)
        sums = jnp.where(lane == j, total, sums)
    high = rounded(peaks)
    middle = rounded(peaks - high)
    low = rounded(peaks - high - middle)
    sum_high = rounded(sums)
    sum_low = rounded(sums - sum_high)
    packed = (
        high + pltpu.roll(middle, HEADS, 1) + pltpu.roll(low, 2 * HEADS, 1)
        + pltpu.roll(sum_high, 3 * HEADS, 1) + pltpu.roll(sum_low, 4 * HEADS, 1)
    )
    o_part[:, F:] = packed.astype(bf16)
    scatter(5, o_part, r_o, s, along_seq)

    all_of(4, r_kv, seq_peer).wait_recv()
    own_keys = turned(slot_sum(r_kv, slice(0, F)), table).astype(bf16)
    own_values = slot_sum(r_kv, slice(F, 2 * F)).astype(bf16)
    causal = lax.broadcasted_iota(jnp.int32, (B, B), 1) <= lax.broadcasted_iota(jnp.int32, (B, B), 0)
    own_lane = lax.broadcasted_iota(jnp.int32, (B, ST), 1)
    own_peaks = jnp.zeros((B, ST), f32)
    own_sums = jnp.zeros((B, ST), f32)
    own_out = []
    for j in range(HEADS):
        cols = slice(j * HD, (j + 1) * HD)
        scores = lax.dot_general(
            queries[:, cols], own_keys[:, cols], (((1,), (1,)), ((), ())), preferred_element_type=f32
        )
        scores = jnp.where(causal, scores, -jnp.inf)
        peak = jnp.max(scores, axis=1, keepdims=True)
        weights = jnp.exp2((scores - peak) * EXP_SCALE)
        total = jnp.sum(weights, axis=1, keepdims=True)
        own_out.append(jnp.dot(weights.astype(bf16), own_values[:, cols], preferred_element_type=f32))
        own_peaks = jnp.where(own_lane == j, peak, own_peaks)
        own_sums = jnp.where(own_lane == j, total, own_sums)

    all_of(5, r_o, seq_peer).wait_recv()
    stats = r_o[:, F:].astype(f32)
    part_peaks = stats + pltpu.roll(stats, ST - HEADS, 1) + pltpu.roll(stats, ST - 2 * HEADS, 1)
    part_sums = pltpu.roll(stats, ST - 3 * HEADS, 1) + pltpu.roll(stats, ST - 4 * HEADS, 1)
    part_peaks = part_peaks.reshape(N, B, ST)
    part_sums = part_sums.reshape(N, B, ST)
    top = jnp.maximum(jnp.max(part_peaks, axis=0), own_peaks)
    factor = jnp.exp2((part_peaks - top[None]) * EXP_SCALE)
    own_factor = jnp.exp2((own_peaks - top) * EXP_SCALE)
    weight_sum = jnp.sum(factor * part_sums, axis=0) + own_factor * own_sums
    for j in range(HEADS):
        cols = slice(j * HD, (j + 1) * HD)
        part = r_o[:, cols].astype(f32).reshape(N, B, HD)
        summed = jnp.sum(part * factor[:, :, j : j + 1], axis=0) + own_out[j] * own_factor[:, j : j + 1]
        att[rows_of(s), cols] = (summed / weight_sum[:, j : j + 1]).astype(bf16)
    spread(6, att, s, along_seq)
    loads[8].wait()
    all_of(6, att, seq_peer).wait_recv()

    out_part[...] = jnp.dot(att[...], wo[...], preferred_element_type=f32).astype(bf16)

    def send_out(d, carry):
        t = lax.rem(s + d, N)

        @pl.when((d > 0) | (s != h))
        def _():
            pltpu.make_async_remote_copy(
                src_ref=out_part.at[rows_of(t)], dst_ref=r_out.at[rows_of(h)],
                send_sem=send_sem.at[7], recv_sem=recv_sem.at[7],
                device_id=(t, s), device_id_type=MESH,
            ).start()

        return carry

    lax.fori_loop(0, N, send_out, 0)

    @pl.when(s == h)
    def _():
        r_out[rows_of(h), :] = out_part[rows_of(h), :]
        all_of(7, r_out, seq_peer, N - 1).wait_recv()

    @pl.when(s != h)
    def _():
        all_of(7, r_out, seq_peer, N).wait_recv()

    out_ref[...] = slot_sum(r_out).astype(bf16)

    for i, ref in enumerate((pick, x_all, q_part, q_all, kv_part, o_part, att)):
        all_of(i, ref, seq_peer).wait_send()

    @pl.when(s == h)
    def _():
        all_of(7, out_part, seq_peer, N - 1).wait_send()

    @pl.when(s != h)
    def _():
        all_of(7, out_part, seq_peer, N).wait_send()


def rotation_table(first, count):
    half = HD // 2
    frequency = 10000.0 ** (-np.arange(half, dtype=np.float64) / half)
    angles = (first + np.arange(count, dtype=np.float64))[:, None] * frequency[None, :]
    cosine, sine = np.cos(angles), np.sin(angles)
    return np.concatenate(
        [np.concatenate([cosine, cosine], 1), np.concatenate([-sine, sine], 1)], 0
    ).astype(np.float32)


def body(gen_ids, embed_rows, w_query, w_key, w_value, w_out, prompt_keys, prompt_values):
    table = jnp.asarray(rotation_table(prompt_keys.shape[0] * N, B))
    tokens = N * B
    wide = lambda width: pltpu.VMEM((tokens, width), bf16)
    block = pltpu.VMEM((F, F), bf16)
    return pl.pallas_call(
        kernel,
        out_shape=jax.ShapeDtypeStruct((B, F), bf16),
        in_specs=[pl.BlockSpec(memory_space=pl.ANY)] * 9,
        out_specs=pl.BlockSpec(memory_space=pltpu.VMEM),
        scratch_shapes=[
            pltpu.VMEM((N, B), jnp.int32), block, block, block, block, block, block, block,
            pltpu.VMEM((2 * B, HD), f32),
            wide(F), wide(F), wide(F), wide(F), wide(F), wide(F), wide(2 * F), wide(2 * F),
            wide(F + ST), wide(F + ST), wide(F), wide(F), wide(F),
            pltpu.SemaphoreType.DMA((9,)),
            pltpu.SemaphoreType.DMA((8,)),
            pltpu.SemaphoreType.DMA((8,)),
        ],
        compiler_params=pltpu.CompilerParams(
            collective_id=0, has_side_effects=True, vmem_limit_bytes=62 * 1024 * 1024
        ),
    )(gen_ids, embed_rows, w_query, w_key, w_value, w_out, prompt_keys, prompt_values, table)


def solution(mesh):
    return jax.shard_map(
        body,
        mesh=mesh,
        in_specs=(
            P(), P("head", "seq"), P("seq", "head"), P("seq", "head"), P("seq", "head"),
            P("head", "seq"), P("seq", "head"), P("seq", "head"),
        ),
        out_specs=P("seq", "head"),
        check_vma=False,
    )
```

```python
import math

import jax
import jax.numpy as jnp
import numpy as np
from jax import lax
from jax.experimental import pallas as pl
from jax.experimental.pallas import tpu as pltpu
from jax.sharding import PartitionSpec as P

MESH = pl.DeviceIdType.MESH
HD = 128
N = 16
B = 16
F = 512
HALF = N * B // 2
YS = 4
PROMPT = 8 * F
CHUNK = 1024
EXP_SCALE = math.log2(math.e) / math.sqrt(HD)
f32 = jnp.float32
bf16 = jnp.bfloat16
EMB_RS, EMB_AG, Q_RS, Q_Z, K_MOVE, V_MOVE, K_PAIR, V_PAIR, KV_RS, KV_Z, O_Z, W_MOVE, W_TURN, ATT_AG, OUT_RS = range(15)


def part(index, size):
    return pl.ds(pl.multiple_of(index * size, size), size)


def rounded(x):
    return x.astype(bf16).astype(f32)


def slot_sum(ref, slots, rows):
    return jnp.sum(ref[...].astype(f32).reshape(slots, rows, ref.shape[-1]), axis=0)


def turned(x, cosine, sine):
    return x * cosine + pltpu.roll(x, HD // 2, 1) * sine


def kernel(
    ids_hbm, e_hbm, wq_hbm, wk_hbm, wv_hbm, wo_hbm, k_hbm, v_hbm, tab_hbm, out_ref,
    ids, emb, wq, wk, wv, tab, keys, values, w_stage, w_all,
    pick, r_emb, x_all, q_part, r_q, q_mine, q_other, kv_part, r_kv, kv_mine, kv_other,
    scores, o_mine, o_other, att, att_all, out_part, r_out,
    load_sem, send_sem, recv_sem,
):
    s = lax.axis_index("seq")
    h = lax.axis_index("head")
    y, zh, c = s // 4, lax.rem(s // 2, 2), lax.rem(s, 2)
    x, zl = h // 4, lax.rem(h, 4)
    sibling = (s + 1 - 2 * c, h)
    antipode = (s + 2 - 4 * zh, h)
    pos = y * 2 + c
    own = lax.rem(s, 4)
    out_self = own == zl

    loads = [
        pltpu.make_async_copy(src, dst, load_sem.at[i])
        for i, (src, dst) in enumerate(
            [
                (ids_hbm, ids), (e_hbm, emb), (wq_hbm, wq), (wk_hbm, wk), (wv_hbm, wv), (tab_hbm, tab),
                (k_hbm.at[:, part(y, HD)], keys.at[part(c * YS + y, F)]),
                (v_hbm.at[:, part(y, HD)], values.at[part(c * YS + y, F)]),
                (wo_hbm.at[part(y, HD)], w_stage.at[part(y, HD)]),
            ]
        )
    ]
    for load in loads:
        load.start()

    barrier = pltpu.get_barrier_semaphore()

    def greet(device):
        pl.semaphore_signal(barrier, inc=1, device_id=device, device_id_type=MESH)

    def in_group(e):
        return ((e // 2) * 4 + zh * 2 + lax.rem(e, 2), h)

    def greet_plane(d, carry):
        greet((s, lax.rem(h + d, N)))
        return carry

    def greet_group(d, carry):
        greet(in_group(lax.rem(pos + d, 8)))
        return carry

    lax.fori_loop(1, N, greet_plane, 0)
    greet(antipode)
    lax.fori_loop(1, 8, greet_group, 0)

    def copy(i, src, dst, device):
        return pltpu.make_async_remote_copy(
            src_ref=src, dst_ref=dst, send_sem=send_sem.at[i], recv_sem=recv_sem.at[i],
            device_id=device, device_id_type=MESH,
        )

    def rows(i, ref, count):
        return copy(i, ref.at[pl.ds(0, count)], ref.at[pl.ds(0, count)], sibling)

    loads[0].wait()
    shifted = (ids[...] - h * F).astype(f32)
    eye = lax.broadcasted_iota(jnp.int32, (B, B), 0) == lax.broadcasted_iota(jnp.int32, (B, B), 1)
    entry = lax.broadcasted_iota(jnp.int32, (B, F), 1).astype(f32)
    chosen = []
    for b in range(N):
        t = (b % 8) * 2 + b // 8
        row = jnp.broadcast_to(shifted[t : t + 1, :], (B, B))
        column = jnp.sum(jnp.where(eye, row, 0.0), axis=1, keepdims=True)
        chosen.append(jnp.where(column == entry, 1.0, 0.0).astype(bf16))
    selector = jnp.concatenate(chosen, axis=0)
    loads[1].wait()
    pick[...] = jnp.dot(selector, emb[...], preferred_element_type=f32).astype(bf16)

    pl.semaphore_wait(barrier, 15 + 7 + 1)

    def send_pick(d, carry):
        j = lax.rem(h + d, N)
        copy(EMB_RS, pick.at[part(j, B)], r_emb.at[part(h, B)], (s, j)).start()
        return carry

    lax.fori_loop(1, N, send_pick, 0)
    r_emb[part(h, B), :] = pick[part(h, B), :]

    def move_prompt(d, carry):
        j = lax.rem(y + d, YS)
        device = (j * 4 + zh * 2 + c, h)
        slot = part(c * YS + y, F)
        copy(K_MOVE, k_hbm.at[:, part(j, HD)], keys.at[slot], device).start()
        copy(V_MOVE, v_hbm.at[:, part(j, HD)], values.at[slot], device).start()
        copy(W_MOVE, wo_hbm.at[part(j, HD)], w_stage.at[part(y, HD)], device).start()
        return carry

    lax.fori_loop(1, YS, move_prompt, 0)

    rows(EMB_RS, r_emb, 15 * B).wait_recv()
    x_all[part(h, B), :] = slot_sum(r_emb, N, B).astype(bf16)

    def send_x(d, carry):
        copy(EMB_AG, x_all.at[part(h, B)], x_all.at[part(h, B)], (s, lax.rem(h + d, N))).start()
        return carry

    lax.fori_loop(1, N, send_x, 0)
    loads[2].wait()
    rows(EMB_AG, x_all, 15 * B).wait_recv()

    projected = jnp.dot(x_all[...], wq[...], preferred_element_type=f32).astype(bf16)
    for j in range(YS):
        q_part[j * 2 * HALF : (j + 1) * 2 * HALF, :] = projected[:, j * HD : (j + 1) * HD]

    def send_q(d, carry):
        e = lax.rem(pos + d, 8)
        copy(Q_RS, q_part.at[part(e, HALF)], r_q.at[part(pos, HALF)], in_group(e)).start()
        return carry

    lax.fori_loop(1, 8, send_q, 0)
    r_q[part(pos, HALF), :] = q_part[part(pos, HALF), :]

    loads[3].wait()
    loads[4].wait()
    for i, w in enumerate((wk, wv)):
        projected = jnp.dot(x_all[...], w[...], preferred_element_type=f32).astype(bf16)
        for j in range(YS):
            for e in range(2):
                first = ((j * 2 + e) * 2 + i) * HALF
                kv_part[first : first + HALF, :] = projected[e * HALF : (e + 1) * HALF, j * HD : (j + 1) * HD]

    def send_kv(d, carry):
        e = lax.rem(pos + d, 8)
        copy(KV_RS, kv_part.at[part(e, 2 * HALF)], r_kv.at[part(pos, 2 * HALF)], in_group(e)).start()
        return carry

    lax.fori_loop(1, 8, send_kv, 0)
    r_kv[part(pos, 2 * HALF), :] = kv_part[part(pos, 2 * HALF), :]

    loads[8].wait()
    rows(W_MOVE, w_stage, 3 * HD).wait_recv()

    def turn_w(d, carry):
        i = lax.rem(x + d, 4)
        copy(W_TURN, w_stage.at[part(i, HD)], w_all.at[part(x, HD)], (s, 4 * i + zl)).start()
        return carry

    lax.fori_loop(1, 4, turn_w, 0)
    w_all[part(x, HD), :] = w_stage[part(x, HD), :]

    loads[6].wait()
    loads[7].wait()
    rows(K_MOVE, keys, 3 * F).wait_recv()
    rows(V_MOVE, values, 3 * F).wait_recv()
    pair_rows = part(c, PROMPT // 2)
    copy(K_PAIR, keys.at[pair_rows], keys.at[pair_rows], sibling).start()
    copy(V_PAIR, values.at[pair_rows], values.at[pair_rows], sibling).start()

    rows(Q_RS, r_q, 7 * HALF).wait_recv()
    q_sum = slot_sum(r_q, 8, HALF)
    q_mine[...] = q_sum.astype(bf16)
    copy(Q_Z, q_mine, q_other, antipode).start()

    rows(KV_RS, r_kv, 14 * HALF).wait_recv()
    kv_sum = slot_sum(r_kv, 8, 2 * HALF)

    kv_mine[...] = kv_sum.astype(bf16)
    copy(KV_Z, kv_mine, kv_other, antipode).start()

    loads[5].wait()
    cosine = jnp.concatenate([tab[:B, :]] * 8, axis=0)
    sine = jnp.concatenate([tab[B:, :]] * 8, axis=0)
    rows(Q_Z, q_other, HALF).wait_recv()
    queries = turned(q_sum + q_other[...].astype(f32), cosine, sine).astype(bf16)

    rows(K_PAIR, keys, PROMPT // 2).wait_recv()
    peak = None
    for i in range(PROMPT // CHUNK):
        block = lax.dot_general(
            queries, keys[i * CHUNK : (i + 1) * CHUNK, :], (((1,), (1,)), ((), ())), preferred_element_type=f32
        )
        scores[:, i * CHUNK : (i + 1) * CHUNK] = block
        top = jnp.max(block, axis=1, keepdims=True)
        peak = top if peak is None else jnp.maximum(peak, top)
    rows(V_PAIR, values, PROMPT // 2).wait_recv()
    weight_sum = jnp.zeros((HALF, 1), f32)
    summed = jnp.zeros((HALF, HD), f32)
    for i in range(PROMPT // CHUNK):
        weights = jnp.exp2((scores[:, i * CHUNK : (i + 1) * CHUNK] - peak) * EXP_SCALE)
        weight_sum += jnp.sum(weights, axis=1, keepdims=True)
        summed += jnp.dot(
            weights.astype(bf16), values[i * CHUNK : (i + 1) * CHUNK, :], preferred_element_type=f32
        )

    lane = lax.broadcasted_iota(jnp.int32, (HALF, HD), 1)
    high = rounded(peak)
    middle = rounded(peak - high)
    sum_high = rounded(weight_sum)
    packed = jnp.zeros((HALF, HD), f32)
    for i, stat in enumerate(
        (high, middle, rounded(peak - high - middle), sum_high, rounded(weight_sum - sum_high))
    ):
        packed = jnp.where(lane == i, stat, packed)
    o_mine[:HALF, :] = summed.astype(bf16)
    o_mine[HALF:, :] = packed.T[:B, :].astype(bf16)
    copy(O_Z, o_mine, o_other, antipode).start()

    rows(KV_Z, kv_other, 2 * HALF).wait_recv()
    both = kv_sum + kv_other[...].astype(f32)
    own_keys = turned(both[:HALF], cosine, sine).astype(bf16)
    own_values = both[HALF:].astype(bf16)
    own_scores = lax.dot_general(queries, own_keys, (((1,), (1,)), ((), ())), preferred_element_type=f32)
    token = lax.broadcasted_iota(jnp.int32, (HALF, HALF), 0)
    other = lax.broadcasted_iota(jnp.int32, (HALF, HALF), 1)
    seen = (token // B == other // B) & (other <= token)
    own_scores = jnp.where(seen, own_scores, -jnp.inf)
    own_peak = jnp.max(own_scores, axis=1, keepdims=True)
    own_weights = jnp.exp2((own_scores - own_peak) * EXP_SCALE)
    own_sum = jnp.sum(own_weights, axis=1, keepdims=True)
    own_out = jnp.dot(own_weights.astype(bf16), own_values, preferred_element_type=f32)

    rows(O_Z, o_other, HALF + B).wait_recv()
    stats = o_other[HALF:, :].astype(f32).T
    far_peak = stats[:, 0:1] + stats[:, 1:2] + stats[:, 2:3]
    far_sum = stats[:, 3:4] + stats[:, 4:5]
    top = jnp.maximum(jnp.maximum(peak, own_peak), far_peak)
    near = jnp.exp2((peak - top) * EXP_SCALE)
    far = jnp.exp2((far_peak - top) * EXP_SCALE)
    mine = jnp.exp2((own_peak - top) * EXP_SCALE)
    total = near * weight_sum + far * far_sum + mine * own_sum
    joined = near * summed + far * o_other[:HALF, :].astype(f32) + mine * own_out
    att[...] = (joined / total).astype(bf16)

    place = x * 2 + c

    def send_att(d, carry):
        e = lax.rem(place + d, 8)
        device = (s - c + lax.rem(e, 2), (e // 2) * 4 + zl)
        copy(ATT_AG, att, att_all.at[part(place, HALF)], device).start()
        return carry

    lax.fori_loop(1, 8, send_att, 0)
    att_all[part(place, HALF), :] = att[...]
    rows(W_TURN, w_all, 3 * HD).wait_recv()
    rows(ATT_AG, att_all, 7 * HALF).wait_recv()

    attended = jnp.concatenate(
        [
            jnp.concatenate([att_all[(i * 2 + e) * HALF : (i * 2 + e + 1) * HALF, :] for i in range(4)], axis=1)
            for e in range(2)
        ],
        axis=0,
    )
    out_part[...] = jnp.dot(attended, w_all[...], preferred_element_type=f32).astype(bf16)
    out_slot = part(y * 4 + zl, B)

    def send_out(d, carry):
        t = lax.rem(s + d, N)
        block = lax.rem(t, 2) * 8 + t // 2

        @pl.when((d > 0) | jnp.logical_not(out_self))
        def _():
            copy(OUT_RS, out_part.at[part(block, B)], r_out.at[out_slot], (t, 4 * x + own)).start()

        return carry

    lax.fori_loop(0, N, send_out, 0)

    @pl.when(out_self)
    def _():
        r_out[out_slot, :] = out_part[part(c * 8 + s // 2, B), :]
        rows(OUT_RS, r_out, 15 * B).wait_recv()

    @pl.when(jnp.logical_not(out_self))
    def _():
        rows(OUT_RS, r_out, 16 * B).wait_recv()

    out_ref[...] = slot_sum(r_out, N, B).astype(bf16)

    rows(EMB_RS, pick, 15 * B).wait_send()
    rows(EMB_AG, x_all, 15 * B).wait_send()
    rows(K_MOVE, keys, 3 * F).wait_send()
    rows(V_MOVE, values, 3 * F).wait_send()
    rows(W_MOVE, w_stage, 3 * HD).wait_send()
    rows(K_PAIR, keys, PROMPT // 2).wait_send()
    rows(V_PAIR, values, PROMPT // 2).wait_send()
    rows(Q_RS, q_part, 7 * HALF).wait_send()
    rows(Q_Z, q_mine, HALF).wait_send()
    rows(KV_RS, kv_part, 14 * HALF).wait_send()
    rows(KV_Z, kv_mine, 2 * HALF).wait_send()
    rows(O_Z, o_mine, HALF + B).wait_send()
    rows(W_TURN, w_stage, 3 * HD).wait_send()
    rows(ATT_AG, att_all, 7 * HALF).wait_send()

    @pl.when(out_self)
    def _():
        rows(OUT_RS, out_part, 15 * B).wait_send()

    @pl.when(jnp.logical_not(out_self))
    def _():
        rows(OUT_RS, out_part, 16 * B).wait_send()


def rotation_table(first, count):
    half = HD // 2
    frequency = 10000.0 ** (-np.arange(half, dtype=np.float64) / half)
    angles = (first + np.arange(count, dtype=np.float64))[:, None] * frequency[None, :]
    cosine, sine = np.cos(angles), np.sin(angles)
    return np.concatenate(
        [np.concatenate([cosine, cosine], 1), np.concatenate([-sine, sine], 1)], 0
    ).astype(np.float32)


def body(gen_ids, embed_rows, w_query, w_key, w_value, w_out, prompt_keys, prompt_values):
    table = jnp.asarray(rotation_table(prompt_keys.shape[0] * N, B))

    def held(count, width=HD, dtype=bf16):
        return pltpu.VMEM((count, width), dtype)

    return pl.pallas_call(
        kernel,
        out_shape=jax.ShapeDtypeStruct((B, F), bf16),
        in_specs=[pl.BlockSpec(memory_space=pl.ANY)] * 9,
        out_specs=pl.BlockSpec(memory_space=pltpu.VMEM),
        scratch_shapes=[
            held(N, B, jnp.int32), held(F, F), held(F, F), held(F, F), held(F, F), held(2 * B, HD, f32),
            held(PROMPT), held(PROMPT), held(F, F), held(F, F),
            held(N * B, F), held(N * B, F), held(N * B, F),
            held(8 * HALF), held(8 * HALF), held(HALF), held(HALF),
            held(16 * HALF), held(16 * HALF), held(2 * HALF), held(2 * HALF),
            held(HALF, PROMPT, f32), held(HALF + B), held(HALF + B),
            held(HALF), held(8 * HALF), held(N * B, F), held(N * B, F),
            pltpu.SemaphoreType.DMA((9,)),
            pltpu.SemaphoreType.DMA((15,)),
            pltpu.SemaphoreType.DMA((15,)),
        ],
        compiler_params=pltpu.CompilerParams(
            collective_id=0, has_side_effects=True, vmem_limit_bytes=62 * 1024 * 1024
        ),
    )(gen_ids, embed_rows, w_query, w_key, w_value, w_out, prompt_keys, prompt_values, table)


def solution(mesh):
    return jax.shard_map(
        body,
        mesh=mesh,
        in_specs=(
            P(), P("head", "seq"), P("seq", "head"), P("seq", "head"), P("seq", "head"),
            P("head", "seq"), P("seq", "head"), P("seq", "head"),
        ),
        out_specs=P("seq", "head"),
        check_vma=False,
    )
```

```python
import math

import jax
import jax.numpy as jnp
import numpy as np
from jax import lax
from jax.experimental import pallas as pl
from jax.experimental.pallas import tpu as pltpu
from jax.sharding import PartitionSpec as P

MESH = pl.DeviceIdType.MESH
HD = 128
N = 16
B = 16
F = 512
CH = N * B // 2
HALF = CH
Q = CH // 2
YS = 4
PROMPT = 8 * F
CHUNK = 1024
EXP_SCALE = math.log2(math.e) / math.sqrt(HD)
f32 = jnp.float32
bf16 = jnp.bfloat16
EMB_RS, K_MOVE, V_MOVE, K_PAIR, V_PAIR, KV_RS, KV_Z, W_MOVE, W_TURN, OUT_RS, KV_PAIR = range(11)
EMB_AG, Q_RS, Q_Z, O_Z, ATT_AG = range(11, 21, 2)


def part(index, size):
    return pl.ds(pl.multiple_of(index * size, size), size)


def rounded(x):
    return x.astype(bf16).astype(f32)


def slot_sum(ref, slots, rows):
    return jnp.sum(ref[...].astype(f32).reshape(slots, rows, ref.shape[-1]), axis=0)


def turned(x, cosine, sine):
    return x * cosine + pltpu.roll(x, HD // 2, 1) * sine


def kernel(
    ids_hbm, e_hbm, wq_hbm, wk_hbm, wv_hbm, wo_hbm, k_hbm, v_hbm, tab_hbm, out_ref,
    ids, emb, wq, wk, wv, tab, keys, values, w_stage, w_all,
    pick, r_emb, x_all, q_part, r_q, q_mine, q_other, kv_part, kv_far, r_kv, kv_mine, kv_other,
    scores, o_mine, o_other, att, att_all, out_part, r_out,
    load_sem, send_sem, recv_sem,
):
    s = lax.axis_index("seq")
    h = lax.axis_index("head")
    y, zh, c = s // 4, lax.rem(s // 2, 2), lax.rem(s, 2)
    x, zl = h // 4, lax.rem(h, 4)
    sibling = (s + 1 - 2 * c, h)
    antipode = (s + 2 - 4 * zh, h)
    pos = y * 2 + c
    own = lax.rem(s, 4)
    out_self = own == zl

    loads = [
        pltpu.make_async_copy(src, dst, load_sem.at[i])
        for i, (src, dst) in enumerate(
            [
                (ids_hbm, ids), (e_hbm, emb), (wq_hbm, wq), (wk_hbm, wk), (wv_hbm, wv), (tab_hbm, tab),
                (k_hbm.at[:, part(y, HD)], keys.at[part(c * YS + y, F)]),
                (v_hbm.at[:, part(y, HD)], values.at[part(c * YS + y, F)]),
                (wo_hbm.at[part(y, HD)], w_stage.at[part(y, HD)]),
            ]
        )
    ]
    for load in loads:
        load.start()

    barrier = pltpu.get_barrier_semaphore()

    def greet(device):
        pl.semaphore_signal(barrier, inc=1, device_id=device, device_id_type=MESH)

    def in_group(e):
        return ((e // 2) * 4 + zh * 2 + lax.rem(e, 2), h)

    def greet_plane(d, carry):
        greet((s, lax.rem(h + d, N)))
        return carry

    def greet_group(d, carry):
        greet(in_group(lax.rem(pos + d, 8)))
        return carry

    lax.fori_loop(1, N, greet_plane, 0)
    greet(antipode)
    lax.fori_loop(1, 8, greet_group, 0)

    def copy(i, src, dst, device):
        return pltpu.make_async_remote_copy(
            src_ref=src, dst_ref=dst, send_sem=send_sem.at[i], recv_sem=recv_sem.at[i],
            device_id=device, device_id_type=MESH,
        )

    def rows(i, ref, count):
        return copy(i, ref.at[pl.ds(0, count)], ref.at[pl.ds(0, count)], sibling)

    loads[0].wait()
    shifted = (ids[...] - h * F).astype(f32)
    eye = lax.broadcasted_iota(jnp.int32, (B, B), 0) == lax.broadcasted_iota(jnp.int32, (B, B), 1)
    entry = lax.broadcasted_iota(jnp.int32, (B, F), 1).astype(f32)
    selectors = []
    for k in range(2):
        chosen = []
        for b in range(8):
            t = (b % 4) * 4 + k * 2 + b // 4
            row = jnp.broadcast_to(shifted[t : t + 1, :], (B, B))
            column = jnp.sum(jnp.where(eye, row, 0.0), axis=1, keepdims=True)
            chosen.append(jnp.where(column == entry, 1.0, 0.0).astype(bf16))
        selectors.append(jnp.concatenate(chosen, axis=0))
    loads[1].wait()
    pick[:CH, :] = jnp.dot(selectors[0], emb[...], preferred_element_type=f32).astype(bf16)

    pl.semaphore_wait(barrier, 15 + 7 + 1)

    mine_k = lax.rem(h, 2)
    mine = mine_k * 8 + h // 2
    for k in range(2):
        if k:
            pick[CH:, :] = jnp.dot(selectors[1], emb[...], preferred_element_type=f32).astype(bf16)

        def send_pick(d, carry, k=k):
            b = lax.rem(h // 2 + d, 8)

            @pl.when((d > 0) | (mine_k != k))
            def _():
                copy(EMB_RS, pick.at[part(k * 8 + b, B)], r_emb.at[part(h, B)], (s, 2 * b + k)).start()

            return carry

        lax.fori_loop(0, 8, send_pick, 0)
    r_emb[part(h, B), :] = pick[part(mine, B), :]

    def move_prompt(d, carry):
        j = lax.rem(y + d, YS)
        device = (j * 4 + zh * 2 + c, h)
        slot = part(c * YS + y, F)
        copy(K_MOVE, k_hbm.at[:, part(j, HD)], keys.at[slot], device).start()
        copy(V_MOVE, v_hbm.at[:, part(j, HD)], values.at[slot], device).start()
        return carry

    lax.fori_loop(1, YS, move_prompt, 0)

    def move_w(d, carry):
        j = lax.rem(y + d, YS)
        device = (j * 4 + zh * 2 + c, h)
        copy(W_MOVE, wo_hbm.at[part(j, HD)], w_stage.at[part(y, HD)], device).start()
        return carry

    lax.fori_loop(1, YS, move_w, 0)

    rows(EMB_RS, r_emb, 15 * B).wait_recv()
    x_all[part(mine, B), :] = slot_sum(r_emb, N, B).astype(bf16)

    def send_x(d, carry):
        copy(EMB_AG + mine_k, x_all.at[part(mine, B)], x_all.at[part(mine, B)], (s, lax.rem(h + d, N))).start()
        return carry

    lax.fori_loop(1, N, send_x, 0)
    loads[2].wait()

    for k in range(2):
        @pl.when(mine_k == k)
        def _(k=k):
            rows(EMB_AG + k, x_all, 7 * B).wait_recv()

        @pl.when(mine_k != k)
        def _(k=k):
            rows(EMB_AG + k, x_all, 8 * B).wait_recv()

        projected = jnp.dot(x_all[k * CH : (k + 1) * CH, :], wq[...], preferred_element_type=f32).astype(bf16)
        for e in range(8):
            q_part[(k * 8 + e) * Q : (k * 8 + e + 1) * Q, :] = projected[
                (e % 2) * Q : (e % 2 + 1) * Q, (e // 2) * HD : (e // 2 + 1) * HD
            ]

        def send_q(d, carry, k=k):
            e = lax.rem(pos + d, 8)
            copy(Q_RS + k, q_part.at[part(k * 8 + e, Q)], r_q.at[part(k * 8 + pos, Q)], in_group(e)).start()
            return carry

        lax.fori_loop(1, 8, send_q, 0)
        r_q[part(k * 8 + pos, Q), :] = q_part[part(k * 8 + pos, Q), :]

    loads[3].wait()
    loads[4].wait()
    for i, w in enumerate((wk, wv)):
        projected = jnp.dot(x_all[...], w[...], preferred_element_type=f32).astype(bf16)
        for e in range(8):
            for k in range(2):
                first = (((e % 2) * YS + e // 2) * 2 + i) * HALF + k * Q
                row = k * CH + (e % 2) * Q
                kv_part[first : first + Q, :] = projected[row : row + Q, (e // 2) * HD : (e // 2 + 1) * HD]
    copy(KV_PAIR, kv_part.at[part(1 - c, 8 * HALF)], kv_far, sibling).start()

    loads[6].wait()
    loads[7].wait()
    rows(K_MOVE, keys, 3 * F).wait_recv()
    rows(V_MOVE, values, 3 * F).wait_recv()
    pair_rows = part(c, PROMPT // 2)
    copy(K_PAIR, keys.at[pair_rows], keys.at[pair_rows], sibling).start()
    copy(V_PAIR, values.at[pair_rows], values.at[pair_rows], sibling).start()

    rows(KV_PAIR, kv_far, 8 * HALF).wait_recv()
    kv_far[...] = (kv_part[part(c, 8 * HALF), :].astype(f32) + kv_far[...].astype(f32)).astype(bf16)

    def send_kv(d, carry):
        j = lax.rem(y + d, YS)
        device = (j * 4 + zh * 2 + c, h)
        copy(KV_RS, kv_far.at[part(j, 2 * HALF)], r_kv.at[part(y, 2 * HALF)], device).start()
        return carry

    lax.fori_loop(1, YS, send_kv, 0)
    r_kv[part(y, 2 * HALF), :] = kv_far[part(y, 2 * HALF), :]

    q_sums = []
    for k in range(2):
        rows(Q_RS + k, r_q, 7 * Q).wait_recv()
        q_sums.append(jnp.sum(r_q[k * 8 * Q : (k + 1) * 8 * Q, :].astype(f32).reshape(8, Q, HD), axis=0))
        q_mine[k * Q : (k + 1) * Q, :] = q_sums[k].astype(bf16)
        copy(Q_Z + k, q_mine.at[part(k, Q)], q_other.at[part(k, Q)], antipode).start()

    rows(KV_RS, r_kv, 6 * HALF).wait_recv()
    kv_sum = slot_sum(r_kv, YS, 2 * HALF)
    kv_mine[...] = kv_sum.astype(bf16)
    copy(KV_Z, kv_mine, kv_other, antipode).start()

    loads[8].wait()
    rows(W_MOVE, w_stage, 3 * HD).wait_recv()

    def turn_w(d, carry):
        i = lax.rem(x + d, 4)
        copy(W_TURN, w_stage.at[part(i, HD)], w_all.at[part(x, HD)], (s, 4 * i + zl)).start()
        return carry

    lax.fori_loop(1, 4, turn_w, 0)
    w_all[part(x, HD), :] = w_stage[part(x, HD), :]

    loads[5].wait()
    cosine = jnp.concatenate([tab[:B, :]] * 8, axis=0)
    sine = jnp.concatenate([tab[B:, :]] * 8, axis=0)
    lane = lax.broadcasted_iota(jnp.int32, (Q, HD), 1)
    found = []
    for k in range(2):
        rows(Q_Z + k, q_other, Q).wait_recv()
        total = q_sums[k] + q_other[k * Q : (k + 1) * Q, :].astype(f32)
        queries = turned(total, cosine[:Q], sine[:Q]).astype(bf16)
        if k == 0:
            rows(K_PAIR, keys, PROMPT // 2).wait_recv()
        peak = None
        for i in range(PROMPT // CHUNK):
            block = lax.dot_general(
                queries, keys[i * CHUNK : (i + 1) * CHUNK, :], (((1,), (1,)), ((), ())), preferred_element_type=f32
            )
            scores[k * Q : (k + 1) * Q, i * CHUNK : (i + 1) * CHUNK] = block
            top = jnp.max(block, axis=1, keepdims=True)
            peak = top if peak is None else jnp.maximum(peak, top)
        if k == 0:
            rows(V_PAIR, values, PROMPT // 2).wait_recv()
        weight_sum = jnp.zeros((Q, 1), f32)
        summed = jnp.zeros((Q, HD), f32)
        for i in range(PROMPT // CHUNK):
            weights = jnp.exp2((scores[k * Q : (k + 1) * Q, i * CHUNK : (i + 1) * CHUNK] - peak) * EXP_SCALE)
            weight_sum += jnp.sum(weights, axis=1, keepdims=True)
            summed += jnp.dot(
                weights.astype(bf16), values[i * CHUNK : (i + 1) * CHUNK, :], preferred_element_type=f32
            )
        high = rounded(peak)
        middle = rounded(peak - high)
        sum_high = rounded(weight_sum)
        packed = jnp.zeros((Q, HD), f32)
        for i, stat in enumerate(
            (high, middle, rounded(peak - high - middle), sum_high, rounded(weight_sum - sum_high))
        ):
            packed = jnp.where(lane == i, stat, packed)
        packed = jnp.concatenate([packed, jnp.zeros((HD - Q, HD), f32)], axis=0)
        first = k * (Q + B)
        o_mine[first : first + Q, :] = summed.astype(bf16)
        o_mine[first + Q : first + Q + B, :] = packed.T[:B, :].astype(bf16)
        copy(O_Z + k, o_mine.at[part(k, Q + B)], o_other.at[part(k, Q + B)], antipode).start()
        found.append((queries, peak, weight_sum, summed))

    rows(KV_Z, kv_other, 2 * HALF).wait_recv()
    both = kv_sum + kv_other[...].astype(f32)
    own_keys = turned(both[:HALF], cosine, sine).astype(bf16)
    own_values = both[HALF:].astype(bf16)
    queries = jnp.concatenate([found[0][0], found[1][0]], axis=0)
    own_scores = lax.dot_general(queries, own_keys, (((1,), (1,)), ((), ())), preferred_element_type=f32)
    token = lax.broadcasted_iota(jnp.int32, (HALF, HALF), 0)
    other = lax.broadcasted_iota(jnp.int32, (HALF, HALF), 1)
    seen = (token // B == other // B) & (other <= token)
    own_scores = jnp.where(seen, own_scores, -jnp.inf)
    own_peak = jnp.max(own_scores, axis=1, keepdims=True)
    own_weights = jnp.exp2((own_scores - own_peak) * EXP_SCALE)
    own_sum = jnp.sum(own_weights, axis=1, keepdims=True)
    own_out = jnp.dot(own_weights.astype(bf16), own_values, preferred_element_type=f32)

    place = x * 2 + c
    for k in range(2):
        rows(O_Z + k, o_other, Q + B).wait_recv()
        _, peak, weight_sum, summed = found[k]
        here = slice(k * Q, (k + 1) * Q)
        first = k * (Q + B)
        stats = o_other[first + Q : first + Q + B, :].astype(f32).T[:Q, :]
        far_peak = stats[:, 0:1] + stats[:, 1:2] + stats[:, 2:3]
        far_sum = stats[:, 3:4] + stats[:, 4:5]
        top = jnp.maximum(jnp.maximum(peak, own_peak[here]), far_peak)
        near = jnp.exp2((peak - top) * EXP_SCALE)
        far = jnp.exp2((far_peak - top) * EXP_SCALE)
        own_factor = jnp.exp2((own_peak[here] - top) * EXP_SCALE)
        total = near * weight_sum + far * far_sum + own_factor * own_sum[here]
        joined = near * summed + far * o_other[first : first + Q, :].astype(f32) + own_factor * own_out[here]
        att[here, :] = (joined / total).astype(bf16)

        def send_att(d, carry, k=k):
            e = lax.rem(place + d, 8)
            device = (s - c + lax.rem(e, 2), (e // 2) * 4 + zl)
            copy(ATT_AG + k, att.at[part(k, Q)], att_all.at[part(k * 8 + place, Q)], device).start()
            return carry

        lax.fori_loop(1, 8, send_att, 0)
        att_all[part(k * 8 + place, Q), :] = att[here, :]

    rows(W_TURN, w_all, 3 * HD).wait_recv()
    out_slot = part(y * 4 + zl, B)
    for k in range(2):
        rows(ATT_AG + k, att_all, 7 * Q).wait_recv()
        attended = jnp.concatenate(
            [
                jnp.concatenate(
                    [att_all[(k * 8 + i * 2 + e) * Q : (k * 8 + i * 2 + e + 1) * Q, :] for i in range(4)], axis=1
                )
                for e in range(2)
            ],
            axis=0,
        )
        out_part[k * CH : (k + 1) * CH, :] = jnp.dot(
            attended, w_all[...], preferred_element_type=f32
        ).astype(bf16)

        def send_out(d, carry, k=k):
            e = lax.rem(pos + d, 8)
            block = k * 8 + lax.rem(e, 2) * 4 + e // 2
            device = ((e // 2) * 4 + k * 2 + lax.rem(e, 2), 4 * x + own)

            @pl.when((d > 0) | (zh != k) | jnp.logical_not(out_self))
            def _():
                copy(OUT_RS, out_part.at[part(block, B)], r_out.at[out_slot], device).start()

            return carry

        lax.fori_loop(0, 8, send_out, 0)

    @pl.when(out_self)
    def _():
        r_out[out_slot, :] = out_part[part(zh * 8 + c * 4 + y, B), :]
        rows(OUT_RS, r_out, 15 * B).wait_recv()

    @pl.when(jnp.logical_not(out_self))
    def _():
        rows(OUT_RS, r_out, 16 * B).wait_recv()

    out_ref[...] = slot_sum(r_out, N, B).astype(bf16)

    rows(EMB_RS, pick, 15 * B).wait_send()
    rows(EMB_AG + mine_k, x_all, 15 * B).wait_send()
    rows(K_MOVE, keys, 3 * F).wait_send()
    rows(V_MOVE, values, 3 * F).wait_send()
    rows(W_MOVE, w_stage, 3 * HD).wait_send()
    rows(K_PAIR, keys, PROMPT // 2).wait_send()
    rows(V_PAIR, values, PROMPT // 2).wait_send()
    for k in range(2):
        rows(Q_RS + k, q_part, 7 * Q).wait_send()
        rows(Q_Z + k, q_mine, Q).wait_send()
        rows(O_Z + k, o_mine, Q + B).wait_send()
        rows(ATT_AG + k, att_all, 7 * Q).wait_send()
    rows(KV_PAIR, kv_part, 8 * HALF).wait_send()
    rows(KV_RS, kv_far, 6 * HALF).wait_send()
    rows(KV_Z, kv_mine, 2 * HALF).wait_send()
    rows(W_TURN, w_stage, 3 * HD).wait_send()

    @pl.when(out_self)
    def _():
        rows(OUT_RS, out_part, 15 * B).wait_send()

    @pl.when(jnp.logical_not(out_self))
    def _():
        rows(OUT_RS, out_part, 16 * B).wait_send()


def rotation_table(first, count):
    half = HD // 2
    frequency = 10000.0 ** (-np.arange(half, dtype=np.float64) / half)
    angles = (first + np.arange(count, dtype=np.float64))[:, None] * frequency[None, :]
    cosine, sine = np.cos(angles), np.sin(angles)
    return np.concatenate(
        [np.concatenate([cosine, cosine], 1), np.concatenate([-sine, sine], 1)], 0
    ).astype(np.float32)


def body(gen_ids, embed_rows, w_query, w_key, w_value, w_out, prompt_keys, prompt_values):
    table = jnp.asarray(rotation_table(prompt_keys.shape[0] * N, B))

    def held(count, width=HD, dtype=bf16):
        return pltpu.VMEM((count, width), dtype)

    return pl.pallas_call(
        kernel,
        out_shape=jax.ShapeDtypeStruct((B, F), bf16),
        in_specs=[pl.BlockSpec(memory_space=pl.ANY)] * 9,
        out_specs=pl.BlockSpec(memory_space=pltpu.VMEM),
        scratch_shapes=[
            held(N, B, jnp.int32), held(F, F), held(F, F), held(F, F), held(F, F), held(2 * B, HD, f32),
            held(PROMPT), held(PROMPT), held(F, F), held(F, F),
            held(N * B, F), held(N * B, F), held(N * B, F),
            held(8 * HALF), held(8 * HALF), held(HALF), held(HALF),
            held(16 * HALF), held(8 * HALF), held(8 * HALF), held(2 * HALF), held(2 * HALF),
            held(HALF, PROMPT, f32), held(HALF + 2 * B), held(HALF + 2 * B),
            held(HALF), held(8 * HALF), held(N * B, F), held(N * B, F),
            pltpu.SemaphoreType.DMA((9,)),
            pltpu.SemaphoreType.DMA((21,)),
            pltpu.SemaphoreType.DMA((21,)),
        ],
        compiler_params=pltpu.CompilerParams(
            collective_id=0, has_side_effects=True, vmem_limit_bytes=62 * 1024 * 1024
        ),
    )(gen_ids, embed_rows, w_query, w_key, w_value, w_out, prompt_keys, prompt_values, table)


def solution(mesh):
    return jax.shard_map(
        body,
        mesh=mesh,
        in_specs=(
            P(), P("head", "seq"), P("seq", "head"), P("seq", "head"), P("seq", "head"),
            P("head", "seq"), P("seq", "head"), P("seq", "head"),
        ),
        out_specs=P("seq", "head"),
        check_vma=False,
    )
```

```python
import math

import jax
import jax.numpy as jnp
import numpy as np
from jax import lax
from jax.experimental import pallas as pl
from jax.experimental.pallas import tpu as pltpu
from jax.sharding import PartitionSpec as P

MESH = pl.DeviceIdType.MESH
HD = 128
N = 16
B = 16
F = 512
CH = N * B // 2
HALF = CH
Q = CH // 2
YS = 4
PROMPT = 8 * F
CHUNK = 1024
EXP_SCALE = math.log2(math.e) / math.sqrt(HD)
f32 = jnp.float32
bf16 = jnp.bfloat16
EMB_RS, K_MOVE, V_MOVE, K_PAIR, V_PAIR, KV_RS, KV_Z, W_MOVE, W_TURN, OUT_RS, KV_PAIR = range(11)
EMB_AG, Q_RS, Q_Z, O_Z, ATT_AG = range(11, 21, 2)


def part(index, size):
    return pl.ds(pl.multiple_of(index * size, size), size)


def rounded(x):
    return x.astype(bf16).astype(f32)


def slot_sum(ref, slots, rows):
    return jnp.sum(ref[...].astype(f32).reshape(slots, rows, ref.shape[-1]), axis=0)


def turned(x, cosine, sine):
    return x * cosine + pltpu.roll(x, HD // 2, 1) * sine


def kernel(
    ids_hbm, e_hbm, wq_hbm, wk_hbm, wv_hbm, wo_hbm, k_hbm, v_hbm, tab_hbm, out_ref,
    ids, emb, wq, wk, wv, tab, keys, values, w_stage, w_all,
    pick, r_emb, x_all, q_part, r_q, q_mine, q_other, kv_part, kv_far, r_kv, kv_mine, kv_other,
    scores, o_mine, o_other, att, att_all, out_part, r_out,
    load_sem, send_sem, recv_sem,
):
    s = lax.axis_index("seq")
    h = lax.axis_index("head")
    y, zh, c = s // 4, lax.rem(s // 2, 2), lax.rem(s, 2)
    x, zl = h // 4, lax.rem(h, 4)
    sibling = (s + 1 - 2 * c, h)
    antipode = (s + 2 - 4 * zh, h)
    pos = y * 2 + c
    own = lax.rem(s, 4)
    out_self = own == zl

    loads = [
        pltpu.make_async_copy(src, dst, load_sem.at[i])
        for i, (src, dst) in enumerate(
            [
                (ids_hbm, ids), (e_hbm, emb), (wq_hbm, wq), (wk_hbm, wk), (wv_hbm, wv), (tab_hbm, tab),
                (k_hbm.at[:, part(y, HD)], keys.at[part(c * YS + y, F)]),
                (v_hbm.at[:, part(y, HD)], values.at[part(c * YS + y, F)]),
                (wo_hbm.at[part(y, HD)], w_stage.at[part(y, HD)]),
            ]
        )
    ]
    for load in loads:
        load.start()

    barrier = pltpu.get_barrier_semaphore()

    def greet(device):
        pl.semaphore_signal(barrier, inc=1, device_id=device, device_id_type=MESH)

    def far_first(base, core):
        return [2 * lax.rem(base + d, 4) + lax.rem(core + e, 2) for d in (2, 1, 3, 0) for e in (1, 0)]

    def in_group(e):
        return ((e // 2) * 4 + zh * 2 + lax.rem(e, 2), h)

    def greet_plane(d, carry):
        greet((s, lax.rem(h + d, N)))
        return carry

    def greet_group(d, carry):
        greet(in_group(lax.rem(pos + d, 8)))
        return carry

    lax.fori_loop(1, N, greet_plane, 0)
    greet(antipode)
    lax.fori_loop(1, 8, greet_group, 0)

    def copy(i, src, dst, device):
        return pltpu.make_async_remote_copy(
            src_ref=src, dst_ref=dst, send_sem=send_sem.at[i], recv_sem=recv_sem.at[i],
            device_id=device, device_id_type=MESH,
        )

    def rows(i, ref, count):
        return copy(i, ref.at[pl.ds(0, count)], ref.at[pl.ds(0, count)], sibling)

    loads[0].wait()
    shifted = (ids[...] - h * F).astype(f32)
    eye = lax.broadcasted_iota(jnp.int32, (B, B), 0) == lax.broadcasted_iota(jnp.int32, (B, B), 1)
    entry = lax.broadcasted_iota(jnp.int32, (B, F), 1).astype(f32)
    selectors = []
    for k in range(2):
        chosen = []
        for b in range(8):
            t = (b % 4) * 4 + k * 2 + b // 4
            row = jnp.broadcast_to(shifted[t : t + 1, :], (B, B))
            column = jnp.sum(jnp.where(eye, row, 0.0), axis=1, keepdims=True)
            chosen.append(jnp.where(column == entry, 1.0, 0.0).astype(bf16))
        selectors.append(jnp.concatenate(chosen, axis=0))
    loads[1].wait()
    pick[:CH, :] = jnp.dot(selectors[0], emb[...], preferred_element_type=f32).astype(bf16)

    pl.semaphore_wait(barrier, 15 + 7 + 1)

    def move_prompt(d, carry):
        j = lax.rem(y + d, YS)
        device = (j * 4 + zh * 2 + c, h)
        slot = part(c * YS + y, F)
        copy(K_MOVE, k_hbm.at[:, part(j, HD)], keys.at[slot], device).start()
        copy(V_MOVE, v_hbm.at[:, part(j, HD)], values.at[slot], device).start()
        return carry

    lax.fori_loop(1, YS, move_prompt, 0)

    def move_w(d, carry):
        j = lax.rem(y + d, YS)
        device = (j * 4 + zh * 2 + c, h)
        copy(W_MOVE, wo_hbm.at[part(j, HD)], w_stage.at[part(y, HD)], device).start()
        return carry

    lax.fori_loop(1, YS, move_w, 0)

    mine_k = lax.rem(h, 2)
    mine = mine_k * 8 + h // 2
    for k in range(2):
        if k:
            pick[CH:, :] = jnp.dot(selectors[1], emb[...], preferred_element_type=f32).astype(bf16)

        for d in (2, 1, 3, 0):
            for far in (1 - zl // 2, zl // 2):
                j = lax.rem(x + d, 4) * 4 + 2 * far + k
                send = copy(EMB_RS, pick.at[part(k * 8 + j // 2, B)], r_emb.at[part(h, B)], (s, j))
                if d:
                    send.start()
                else:
                    pl.when(j != h)(send.start)
    r_emb[part(h, B), :] = pick[part(mine, B), :]

    rows(EMB_RS, r_emb, 15 * B).wait_recv()
    x_all[part(mine, B), :] = slot_sum(r_emb, N, B).astype(bf16)

    for d in (2, 1, 3, 0):
        for z in (3 - zl, lax.rem(zl + 2, 4), zl + 1 - 2 * lax.rem(zl, 2), zl)[: 4 if d else 3]:
            device = (s, lax.rem(x + d, 4) * 4 + z)
            copy(EMB_AG + mine_k, x_all.at[part(mine, B)], x_all.at[part(mine, B)], device).start()
    loads[2].wait()

    for k in range(2):
        @pl.when(mine_k == k)
        def _(k=k):
            rows(EMB_AG + k, x_all, 7 * B).wait_recv()

        @pl.when(mine_k != k)
        def _(k=k):
            rows(EMB_AG + k, x_all, 8 * B).wait_recv()

        projected = jnp.dot(x_all[k * CH : (k + 1) * CH, :], wq[...], preferred_element_type=f32).astype(bf16)
        for e in range(8):
            q_part[(k * 8 + e) * Q : (k * 8 + e + 1) * Q, :] = projected[
                (e % 2) * Q : (e % 2 + 1) * Q, (e // 2) * HD : (e // 2 + 1) * HD
            ]

        for e in far_first(y, c)[:7]:
            copy(Q_RS + k, q_part.at[part(k * 8 + e, Q)], r_q.at[part(k * 8 + pos, Q)], in_group(e)).start()
        r_q[part(k * 8 + pos, Q), :] = q_part[part(k * 8 + pos, Q), :]

    loads[3].wait()
    loads[4].wait()
    for i, w in enumerate((wk, wv)):
        projected = jnp.dot(x_all[...], w[...], preferred_element_type=f32).astype(bf16)
        for e in range(8):
            for k in range(2):
                first = (((e % 2) * YS + e // 2) * 2 + i) * HALF + k * Q
                row = k * CH + (e % 2) * Q
                kv_part[first : first + Q, :] = projected[row : row + Q, (e // 2) * HD : (e // 2 + 1) * HD]
    copy(KV_PAIR, kv_part.at[part(1 - c, 8 * HALF)], kv_far, sibling).start()

    rows(KV_PAIR, kv_far, 8 * HALF).wait_recv()
    kv_far[...] = (kv_part[part(c, 8 * HALF), :].astype(f32) + kv_far[...].astype(f32)).astype(bf16)

    def send_kv(d, carry):
        j = lax.rem(y + d, YS)
        device = (j * 4 + zh * 2 + c, h)
        copy(KV_RS, kv_far.at[part(j, 2 * HALF)], r_kv.at[part(y, 2 * HALF)], device).start()
        return carry

    lax.fori_loop(1, YS, send_kv, 0)
    r_kv[part(y, 2 * HALF), :] = kv_far[part(y, 2 * HALF), :]

    q_sums = []
    for k in range(2):
        rows(Q_RS + k, r_q, 7 * Q).wait_recv()
        q_sums.append(jnp.sum(r_q[k * 8 * Q : (k + 1) * 8 * Q, :].astype(f32).reshape(8, Q, HD), axis=0))
        q_mine[k * Q : (k + 1) * Q, :] = q_sums[k].astype(bf16)
        copy(Q_Z + k, q_mine.at[part(k, Q)], q_other.at[part(k, Q)], antipode).start()

    loads[6].wait()
    loads[7].wait()
    rows(K_MOVE, keys, 3 * F).wait_recv()
    rows(V_MOVE, values, 3 * F).wait_recv()
    pair_rows = part(c, PROMPT // 2)
    copy(K_PAIR, keys.at[pair_rows], keys.at[pair_rows], sibling).start()
    copy(V_PAIR, values.at[pair_rows], values.at[pair_rows], sibling).start()

    loads[8].wait()
    rows(W_MOVE, w_stage, 3 * HD).wait_recv()

    def turn_w(d, carry):
        i = lax.rem(x + d, 4)
        copy(W_TURN, w_stage.at[part(i, HD)], w_all.at[part(x, HD)], (s, 4 * i + zl)).start()
        return carry

    lax.fori_loop(1, 4, turn_w, 0)
    w_all[part(x, HD), :] = w_stage[part(x, HD), :]

    rows(KV_RS, r_kv, 6 * HALF).wait_recv()
    kv_sum = slot_sum(r_kv, YS, 2 * HALF)
    kv_mine[...] = kv_sum.astype(bf16)
    copy(KV_Z, kv_mine, kv_other, antipode).start()

    loads[5].wait()
    cosine = jnp.concatenate([tab[:B, :]] * 8, axis=0)
    sine = jnp.concatenate([tab[B:, :]] * 8, axis=0)
    lane = lax.broadcasted_iota(jnp.int32, (Q, HD), 1)
    found = []
    for k in range(2):
        rows(Q_Z + k, q_other, Q).wait_recv()
        total = q_sums[k] + q_other[k * Q : (k + 1) * Q, :].astype(f32)
        queries = turned(total, cosine[:Q], sine[:Q]).astype(bf16)
        if k == 0:
            rows(K_PAIR, keys, PROMPT // 2).wait_recv()
        peak = None
        for i in range(PROMPT // CHUNK):
            block = lax.dot_general(
                queries, keys[i * CHUNK : (i + 1) * CHUNK, :], (((1,), (1,)), ((), ())), preferred_element_type=f32
            )
            scores[k * Q : (k + 1) * Q, i * CHUNK : (i + 1) * CHUNK] = block
            top = jnp.max(block, axis=1, keepdims=True)
            peak = top if peak is None else jnp.maximum(peak, top)
        if k == 0:
            rows(V_PAIR, values, PROMPT // 2).wait_recv()
        weight_sum = jnp.zeros((Q, 1), f32)
        summed = jnp.zeros((Q, HD), f32)
        for i in range(PROMPT // CHUNK):
            weights = jnp.exp2((scores[k * Q : (k + 1) * Q, i * CHUNK : (i + 1) * CHUNK] - peak) * EXP_SCALE)
            weight_sum += jnp.sum(weights, axis=1, keepdims=True)
            summed += jnp.dot(
                weights.astype(bf16), values[i * CHUNK : (i + 1) * CHUNK, :], preferred_element_type=f32
            )
        high = rounded(peak)
        middle = rounded(peak - high)
        sum_high = rounded(weight_sum)
        packed = jnp.zeros((Q, HD), f32)
        for i, stat in enumerate(
            (high, middle, rounded(peak - high - middle), sum_high, rounded(weight_sum - sum_high))
        ):
            packed = jnp.where(lane == i, stat, packed)
        packed = jnp.concatenate([packed, jnp.zeros((HD - Q, HD), f32)], axis=0)
        first = k * (Q + B)
        o_mine[first : first + Q, :] = summed.astype(bf16)
        o_mine[first + Q : first + Q + B, :] = packed.T[:B, :].astype(bf16)
        copy(O_Z + k, o_mine.at[part(k, Q + B)], o_other.at[part(k, Q + B)], antipode).start()
        found.append((queries, peak, weight_sum, summed))

    rows(KV_Z, kv_other, 2 * HALF).wait_recv()
    both = kv_sum + kv_other[...].astype(f32)
    own_keys = turned(both[:HALF], cosine, sine).astype(bf16)
    own_values = both[HALF:].astype(bf16)
    queries = jnp.concatenate([found[0][0], found[1][0]], axis=0)
    own_scores = lax.dot_general(queries, own_keys, (((1,), (1,)), ((), ())), preferred_element_type=f32)
    token = lax.broadcasted_iota(jnp.int32, (HALF, HALF), 0)
    other = lax.broadcasted_iota(jnp.int32, (HALF, HALF), 1)
    seen = (token // B == other // B) & (other <= token)
    own_scores = jnp.where(seen, own_scores, -jnp.inf)
    own_peak = jnp.max(own_scores, axis=1, keepdims=True)
    own_weights = jnp.exp2((own_scores - own_peak) * EXP_SCALE)
    own_sum = jnp.sum(own_weights, axis=1, keepdims=True)
    own_out = jnp.dot(own_weights.astype(bf16), own_values, preferred_element_type=f32)

    place = x * 2 + c
    for k in range(2):
        rows(O_Z + k, o_other, Q + B).wait_recv()
        _, peak, weight_sum, summed = found[k]
        here = slice(k * Q, (k + 1) * Q)
        first = k * (Q + B)
        stats = o_other[first + Q : first + Q + B, :].astype(f32).T[:Q, :]
        far_peak = stats[:, 0:1] + stats[:, 1:2] + stats[:, 2:3]
        far_sum = stats[:, 3:4] + stats[:, 4:5]
        top = jnp.maximum(jnp.maximum(peak, own_peak[here]), far_peak)
        near = jnp.exp2((peak - top) * EXP_SCALE)
        far = jnp.exp2((far_peak - top) * EXP_SCALE)
        own_factor = jnp.exp2((own_peak[here] - top) * EXP_SCALE)
        total = near * weight_sum + far * far_sum + own_factor * own_sum[here]
        joined = near * summed + far * o_other[first : first + Q, :].astype(f32) + own_factor * own_out[here]
        att[here, :] = (joined / total).astype(bf16)

        for e in far_first(x, c)[:7]:
            device = (s - c + lax.rem(e, 2), (e // 2) * 4 + zl)
            copy(ATT_AG + k, att.at[part(k, Q)], att_all.at[part(k * 8 + place, Q)], device).start()
        att_all[part(k * 8 + place, Q), :] = att[here, :]

    rows(W_TURN, w_all, 3 * HD).wait_recv()
    out_slot = part(y * 4 + zl, B)
    for k in range(2):
        rows(ATT_AG + k, att_all, 7 * Q).wait_recv()
        attended = jnp.concatenate(
            [
                jnp.concatenate(
                    [att_all[(k * 8 + i * 2 + e) * Q : (k * 8 + i * 2 + e + 1) * Q, :] for i in range(4)], axis=1
                )
                for e in range(2)
            ],
            axis=0,
        )
        out_part[k * CH : (k + 1) * CH, :] = jnp.dot(
            attended, w_all[...], preferred_element_type=f32
        ).astype(bf16)

        for n, e in enumerate(far_first(y, c)):
            block = k * 8 + lax.rem(e, 2) * 4 + e // 2
            device = ((e // 2) * 4 + k * 2 + lax.rem(e, 2), 4 * x + own)
            send = copy(OUT_RS, out_part.at[part(block, B)], r_out.at[out_slot], device)
            if n < 7:
                send.start()
            else:
                pl.when((zh != k) | jnp.logical_not(out_self))(send.start)

    rows(EMB_RS, pick, 15 * B).wait_send()
    rows(EMB_AG + mine_k, x_all, 15 * B).wait_send()
    rows(K_MOVE, keys, 3 * F).wait_send()
    rows(V_MOVE, values, 3 * F).wait_send()
    rows(W_MOVE, w_stage, 3 * HD).wait_send()
    rows(K_PAIR, keys, PROMPT // 2).wait_send()
    rows(V_PAIR, values, PROMPT // 2).wait_send()
    for k in range(2):
        rows(Q_RS + k, q_part, 7 * Q).wait_send()
        rows(Q_Z + k, q_mine, Q).wait_send()
        rows(O_Z + k, o_mine, Q + B).wait_send()
        rows(ATT_AG + k, att_all, 7 * Q).wait_send()
    rows(KV_PAIR, kv_part, 8 * HALF).wait_send()
    rows(KV_RS, kv_far, 6 * HALF).wait_send()
    rows(KV_Z, kv_mine, 2 * HALF).wait_send()
    rows(W_TURN, w_stage, 3 * HD).wait_send()


    @pl.when(out_self)
    def _():
        r_out[out_slot, :] = out_part[part(zh * 8 + c * 4 + y, B), :]
        rows(OUT_RS, r_out, 15 * B).wait_recv()

    @pl.when(jnp.logical_not(out_self))
    def _():
        rows(OUT_RS, r_out, 16 * B).wait_recv()

    out_ref[...] = slot_sum(r_out, N, B).astype(bf16)

    @pl.when(out_self)
    def _():
        rows(OUT_RS, out_part, 15 * B).wait_send()

    @pl.when(jnp.logical_not(out_self))
    def _():
        rows(OUT_RS, out_part, 16 * B).wait_send()


def rotation_table(first, count):
    half = HD // 2
    frequency = 10000.0 ** (-np.arange(half, dtype=np.float64) / half)
    angles = (first + np.arange(count, dtype=np.float64))[:, None] * frequency[None, :]
    cosine, sine = np.cos(angles), np.sin(angles)
    return np.concatenate(
        [np.concatenate([cosine, cosine], 1), np.concatenate([-sine, sine], 1)], 0
    ).astype(np.float32)


def body(gen_ids, embed_rows, w_query, w_key, w_value, w_out, prompt_keys, prompt_values):
    table = jnp.asarray(rotation_table(prompt_keys.shape[0] * N, B))

    def held(count, width=HD, dtype=bf16):
        return pltpu.VMEM((count, width), dtype)

    return pl.pallas_call(
        kernel,
        out_shape=jax.ShapeDtypeStruct((B, F), bf16),
        in_specs=[pl.BlockSpec(memory_space=pl.ANY)] * 9,
        out_specs=pl.BlockSpec(memory_space=pltpu.VMEM),
        scratch_shapes=[
            held(N, B, jnp.int32), held(F, F), held(F, F), held(F, F), held(F, F), held(2 * B, HD, f32),
            held(PROMPT), held(PROMPT), held(F, F), held(F, F),
            held(N * B, F), held(N * B, F), held(N * B, F),
            held(8 * HALF), held(8 * HALF), held(HALF), held(HALF),
            held(16 * HALF), held(8 * HALF), held(8 * HALF), held(2 * HALF), held(2 * HALF),
            held(HALF, PROMPT, f32), held(HALF + 2 * B), held(HALF + 2 * B),
            held(HALF), held(8 * HALF), held(N * B, F), held(N * B, F),
            pltpu.SemaphoreType.DMA((9,)),
            pltpu.SemaphoreType.DMA((21,)),
            pltpu.SemaphoreType.DMA((21,)),
        ],
        compiler_params=pltpu.CompilerParams(
            collective_id=0, has_side_effects=True, vmem_limit_bytes=62 * 1024 * 1024
        ),
    )(gen_ids, embed_rows, w_query, w_key, w_value, w_out, prompt_keys, prompt_values, table)


def solution(mesh):
    return jax.shard_map(
        body,
        mesh=mesh,
        in_specs=(
            P(), P("head", "seq"), P("seq", "head"), P("seq", "head"), P("seq", "head"),
            P("head", "seq"), P("seq", "head"), P("seq", "head"),
        ),
        out_specs=P("seq", "head"),
        check_vma=False,
    )
```

```python
import math

import jax
import jax.numpy as jnp
import numpy as np
from jax import lax
from jax.experimental import pallas as pl
from jax.experimental.pallas import tpu as pltpu
from jax.sharding import PartitionSpec as P

MESH = pl.DeviceIdType.MESH
HD = 128
N = 16
B = 16
F = 512
CH = N * B // 2
HALF = CH
Q = CH // 2
YS = 4
PROMPT = 8 * F
CHUNK = 1024
EXP_SCALE = math.log2(math.e) / math.sqrt(HD)
f32 = jnp.float32
bf16 = jnp.bfloat16
EMB_RS, K_MOVE, V_MOVE, K_PAIR, V_PAIR, KV_RS, KV_Z, W_MOVE, W_TURN, OUT_RS, KV_PAIR = range(11)
EMB_AG, Q_RS, Q_Z, O_Z, ATT_AG = range(11, 21, 2)


def part(index, size):
    return pl.ds(pl.multiple_of(index * size, size), size)


def rounded(x):
    return x.astype(bf16).astype(f32)


def slot_sum(ref, slots, rows):
    return jnp.sum(ref[...].astype(f32).reshape(slots, rows, ref.shape[-1]), axis=0)


def turned(x, cosine, sine):
    return x * cosine + pltpu.roll(x, HD // 2, 1) * sine


def kernel(
    ids_hbm, e_hbm, wq_hbm, wk_hbm, wv_hbm, wo_hbm, k_hbm, v_hbm, tab_hbm, out_ref,
    ids, emb, wq, wk, wv, tab, keys, values, w_stage, w_all,
    pick, r_emb, x_all, q_part, r_q, q_mine, q_other, kv_part, kv_far, r_kv, kv_mine, kv_other,
    scores, o_mine, o_other, att, att_all, out_part, r_out,
    load_sem, send_sem, recv_sem,
):
    s = lax.axis_index("seq")
    h = lax.axis_index("head")
    y, zh, c = s // 4, lax.rem(s // 2, 2), lax.rem(s, 2)
    x, zl = h // 4, lax.rem(h, 4)
    sibling = (s + 1 - 2 * c, h)
    antipode = (s + 2 - 4 * zh, h)
    pos = y * 2 + c
    own = lax.rem(s, 4)
    out_self = own == zl

    loads = [
        pltpu.make_async_copy(src, dst, load_sem.at[i])
        for i, (src, dst) in enumerate(
            [
                (ids_hbm, ids), (e_hbm, emb), (wq_hbm, wq), (wk_hbm, wk), (wv_hbm, wv), (tab_hbm, tab),
                (k_hbm.at[:, part(y, HD)], keys.at[part(c * YS + y, F)]),
                (v_hbm.at[:, part(y, HD)], values.at[part(c * YS + y, F)]),
                (wo_hbm.at[part(y, HD)], w_stage.at[part(y, HD)]),
            ]
        )
    ]
    for load in loads[:2]:
        load.start()

    barrier = pltpu.get_barrier_semaphore()

    def greet(device):
        pl.semaphore_signal(barrier, inc=1, device_id=device, device_id_type=MESH)

    def far_first(base, core):
        return [2 * lax.rem(base + d, 4) + lax.rem(core + e, 2) for d in (2, 1, 3, 0) for e in (1, 0)]

    def in_group(e):
        return ((e // 2) * 4 + zh * 2 + lax.rem(e, 2), h)

    for d in (2, 1, 3, 0):
        for z in (3 - zl, lax.rem(zl + 2, 4), zl + 1 - 2 * lax.rem(zl, 2), zl)[: 4 if d else 3]:
            greet((s, lax.rem(x + d, 4) * 4 + z))
    greet(antipode)
    for e in far_first(y, c)[:7]:
        greet(in_group(e))

    for load in loads[2:]:
        load.start()

    def copy(i, src, dst, device):
        return pltpu.make_async_remote_copy(
            src_ref=src, dst_ref=dst, send_sem=send_sem.at[i], recv_sem=recv_sem.at[i],
            device_id=device, device_id_type=MESH,
        )

    def rows(i, ref, count):
        return copy(i, ref.at[pl.ds(0, count)], ref.at[pl.ds(0, count)], sibling)

    loads[0].wait()
    shifted = (ids[...] - h * F).astype(f32)
    eye = lax.broadcasted_iota(jnp.int32, (B, B), 0) == lax.broadcasted_iota(jnp.int32, (B, B), 1)
    entry = lax.broadcasted_iota(jnp.int32, (B, F), 1).astype(f32)
    selectors = []
    for k in range(2):
        chosen = []
        for b in range(8):
            t = (b % 4) * 4 + k * 2 + b // 4
            row = jnp.broadcast_to(shifted[t : t + 1, :], (B, B))
            column = jnp.sum(jnp.where(eye, row, 0.0), axis=1, keepdims=True)
            chosen.append(jnp.where(column == entry, 1.0, 0.0).astype(bf16))
        selectors.append(jnp.concatenate(chosen, axis=0))
    loads[1].wait()
    pick[:CH, :] = jnp.dot(selectors[0], emb[...], preferred_element_type=f32).astype(bf16)

    pl.semaphore_wait(barrier, 15 + 7 + 1)

    def move_prompt(d, carry):
        j = lax.rem(y + d, YS)
        device = (j * 4 + zh * 2 + c, h)
        slot = part(c * YS + y, F)
        copy(K_MOVE, k_hbm.at[:, part(j, HD)], keys.at[slot], device).start()
        copy(V_MOVE, v_hbm.at[:, part(j, HD)], values.at[slot], device).start()
        return carry

    for d in (2, 1, 3):
        move_prompt(d, 0)

    def move_w(d, carry):
        j = lax.rem(y + d, YS)
        device = (j * 4 + zh * 2 + c, h)
        copy(W_MOVE, wo_hbm.at[part(j, HD)], w_stage.at[part(y, HD)], device).start()
        return carry

    for d in (2, 1, 3):
        move_w(d, 0)

    mine_k = lax.rem(h, 2)
    mine = mine_k * 8 + h // 2
    for k in range(2):
        if k:
            pick[CH:, :] = jnp.dot(selectors[1], emb[...], preferred_element_type=f32).astype(bf16)

        for d in (2, 1, 3, 0):
            for far in (1 - zl // 2, zl // 2):
                j = lax.rem(x + d, 4) * 4 + 2 * far + k
                send = copy(EMB_RS, pick.at[part(k * 8 + j // 2, B)], r_emb.at[part(h, B)], (s, j))
                if d:
                    send.start()
                else:
                    pl.when(j != h)(send.start)
    r_emb[part(h, B), :] = pick[part(mine, B), :]

    rows(EMB_RS, r_emb, 15 * B).wait_recv()
    x_all[part(mine, B), :] = slot_sum(r_emb, N, B).astype(bf16)

    for d in (2, 1, 3, 0):
        for z in (3 - zl, lax.rem(zl + 2, 4), zl + 1 - 2 * lax.rem(zl, 2), zl)[: 4 if d else 3]:
            device = (s, lax.rem(x + d, 4) * 4 + z)
            copy(EMB_AG + mine_k, x_all.at[part(mine, B)], x_all.at[part(mine, B)], device).start()
    loads[2].wait()

    for k in range(2):
        @pl.when(mine_k == k)
        def _(k=k):
            rows(EMB_AG + k, x_all, 7 * B).wait_recv()

        @pl.when(mine_k != k)
        def _(k=k):
            rows(EMB_AG + k, x_all, 8 * B).wait_recv()

        projected = jnp.dot(x_all[k * CH : (k + 1) * CH, :], wq[...], preferred_element_type=f32).astype(bf16)
        for e in range(8):
            q_part[(k * 8 + e) * Q : (k * 8 + e + 1) * Q, :] = projected[
                (e % 2) * Q : (e % 2 + 1) * Q, (e // 2) * HD : (e // 2 + 1) * HD
            ]

        for e in far_first(y, c)[:7]:
            copy(Q_RS + k, q_part.at[part(k * 8 + e, Q)], r_q.at[part(k * 8 + pos, Q)], in_group(e)).start()
        r_q[part(k * 8 + pos, Q), :] = q_part[part(k * 8 + pos, Q), :]

    loads[3].wait()
    loads[4].wait()
    for i, w in enumerate((wk, wv)):
        projected = jnp.dot(x_all[...], w[...], preferred_element_type=f32).astype(bf16)
        for e in range(8):
            for k in range(2):
                first = (((e % 2) * YS + e // 2) * 2 + i) * HALF + k * Q
                row = k * CH + (e % 2) * Q
                kv_part[first : first + Q, :] = projected[row : row + Q, (e // 2) * HD : (e // 2 + 1) * HD]
    copy(KV_PAIR, kv_part.at[part(1 - c, 8 * HALF)], kv_far, sibling).start()

    rows(KV_PAIR, kv_far, 8 * HALF).wait_recv()
    kv_far[...] = (kv_part[part(c, 8 * HALF), :].astype(f32) + kv_far[...].astype(f32)).astype(bf16)

    def send_kv(d, carry):
        j = lax.rem(y + d, YS)
        device = (j * 4 + zh * 2 + c, h)
        copy(KV_RS, kv_far.at[part(j, 2 * HALF)], r_kv.at[part(y, 2 * HALF)], device).start()
        return carry

    for d in (2, 1, 3):
        send_kv(d, 0)
    r_kv[part(y, 2 * HALF), :] = kv_far[part(y, 2 * HALF), :]

    q_sums = []
    for k in range(2):
        rows(Q_RS + k, r_q, 7 * Q).wait_recv()
        q_sums.append(jnp.sum(r_q[k * 8 * Q : (k + 1) * 8 * Q, :].astype(f32).reshape(8, Q, HD), axis=0))
        q_mine[k * Q : (k + 1) * Q, :] = q_sums[k].astype(bf16)
        copy(Q_Z + k, q_mine.at[part(k, Q)], q_other.at[part(k, Q)], antipode).start()

    loads[6].wait()
    loads[7].wait()
    rows(K_MOVE, keys, 3 * F).wait_recv()
    rows(V_MOVE, values, 3 * F).wait_recv()
    pair_rows = part(c, PROMPT // 2)
    copy(K_PAIR, keys.at[pair_rows], keys.at[pair_rows], sibling).start()
    copy(V_PAIR, values.at[pair_rows], values.at[pair_rows], sibling).start()

    loads[8].wait()
    rows(W_MOVE, w_stage, 3 * HD).wait_recv()

    def turn_w(d, carry):
        i = lax.rem(x + d, 4)
        copy(W_TURN, w_stage.at[part(i, HD)], w_all.at[part(x, HD)], (s, 4 * i + zl)).start()
        return carry

    for d in (2, 1, 3):
        turn_w(d, 0)
    w_all[part(x, HD), :] = w_stage[part(x, HD), :]

    rows(KV_RS, r_kv, 6 * HALF).wait_recv()
    kv_sum = slot_sum(r_kv, YS, 2 * HALF)
    kv_mine[...] = kv_sum.astype(bf16)
    copy(KV_Z, kv_mine, kv_other, antipode).start()

    loads[5].wait()
    cosine = jnp.concatenate([tab[:B, :]] * 8, axis=0)
    sine = jnp.concatenate([tab[B:, :]] * 8, axis=0)
    lane = lax.broadcasted_iota(jnp.int32, (Q, HD), 1)
    found = []
    for k in range(2):
        rows(Q_Z + k, q_other, Q).wait_recv()
        total = q_sums[k] + q_other[k * Q : (k + 1) * Q, :].astype(f32)
        queries = turned(total, cosine[:Q], sine[:Q]).astype(bf16)
        if k == 0:
            rows(K_PAIR, keys, PROMPT // 2).wait_recv()
        peak = None
        for i in range(PROMPT // CHUNK):
            block = lax.dot_general(
                queries, keys[i * CHUNK : (i + 1) * CHUNK, :], (((1,), (1,)), ((), ())), preferred_element_type=f32
            )
            scores[k * Q : (k + 1) * Q, i * CHUNK : (i + 1) * CHUNK] = block
            top = jnp.max(block, axis=1, keepdims=True)
            peak = top if peak is None else jnp.maximum(peak, top)
        if k == 0:
            rows(V_PAIR, values, PROMPT // 2).wait_recv()
        weight_sum = jnp.zeros((Q, 1), f32)
        summed = jnp.zeros((Q, HD), f32)
        for i in range(PROMPT // CHUNK):
            weights = jnp.exp2((scores[k * Q : (k + 1) * Q, i * CHUNK : (i + 1) * CHUNK] - peak) * EXP_SCALE)
            weight_sum += jnp.sum(weights, axis=1, keepdims=True)
            summed += jnp.dot(
                weights.astype(bf16), values[i * CHUNK : (i + 1) * CHUNK, :], preferred_element_type=f32
            )
        high = rounded(peak)
        middle = rounded(peak - high)
        sum_high = rounded(weight_sum)
        packed = jnp.zeros((Q, HD), f32)
        for i, stat in enumerate(
            (high, middle, rounded(peak - high - middle), sum_high, rounded(weight_sum - sum_high))
        ):
            packed = jnp.where(lane == i, stat, packed)
        packed = jnp.concatenate([packed, jnp.zeros((HD - Q, HD), f32)], axis=0)
        first = k * (Q + B)
        o_mine[first : first + Q, :] = summed.astype(bf16)
        o_mine[first + Q : first + Q + B, :] = packed.T[:B, :].astype(bf16)
        copy(O_Z + k, o_mine.at[part(k, Q + B)], o_other.at[part(k, Q + B)], antipode).start()
        found.append((queries, peak, weight_sum, summed))

    rows(KV_Z, kv_other, 2 * HALF).wait_recv()
    both = kv_sum + kv_other[...].astype(f32)
    own_keys = turned(both[:HALF], cosine, sine).astype(bf16)
    own_values = both[HALF:].astype(bf16)
    queries = jnp.concatenate([found[0][0], found[1][0]], axis=0)
    own_scores = lax.dot_general(queries, own_keys, (((1,), (1,)), ((), ())), preferred_element_type=f32)
    token = lax.broadcasted_iota(jnp.int32, (HALF, HALF), 0)
    other = lax.broadcasted_iota(jnp.int32, (HALF, HALF), 1)
    seen = (token // B == other // B) & (other <= token)
    own_scores = jnp.where(seen, own_scores, -jnp.inf)
    own_peak = jnp.max(own_scores, axis=1, keepdims=True)
    own_weights = jnp.exp2((own_scores - own_peak) * EXP_SCALE)
    own_sum = jnp.sum(own_weights, axis=1, keepdims=True)
    own_out = jnp.dot(own_weights.astype(bf16), own_values, preferred_element_type=f32)

    place = x * 2 + c
    for k in range(2):
        rows(O_Z + k, o_other, Q + B).wait_recv()
        _, peak, weight_sum, summed = found[k]
        here = slice(k * Q, (k + 1) * Q)
        first = k * (Q + B)
        stats = o_other[first + Q : first + Q + B, :].astype(f32).T[:Q, :]
        far_peak = stats[:, 0:1] + stats[:, 1:2] + stats[:, 2:3]
        far_sum = stats[:, 3:4] + stats[:, 4:5]
        top = jnp.maximum(jnp.maximum(peak, own_peak[here]), far_peak)
        near = jnp.exp2((peak - top) * EXP_SCALE)
        far = jnp.exp2((far_peak - top) * EXP_SCALE)
        own_factor = jnp.exp2((own_peak[here] - top) * EXP_SCALE)
        total = near * weight_sum + far * far_sum + own_factor * own_sum[here]
        joined = near * summed + far * o_other[first : first + Q, :].astype(f32) + own_factor * own_out[here]
        att[here, :] = (joined / total).astype(bf16)

        for e in far_first(x, c)[:7]:
            device = (s - c + lax.rem(e, 2), (e // 2) * 4 + zl)
            copy(ATT_AG + k, att.at[part(k, Q)], att_all.at[part(k * 8 + place, Q)], device).start()
        att_all[part(k * 8 + place, Q), :] = att[here, :]

    rows(W_TURN, w_all, 3 * HD).wait_recv()
    out_slot = part(y * 4 + zl, B)
    for k in range(2):
        rows(ATT_AG + k, att_all, 7 * Q).wait_recv()
        attended = jnp.concatenate(
            [
                jnp.concatenate(
                    [att_all[(k * 8 + i * 2 + e) * Q : (k * 8 + i * 2 + e + 1) * Q, :] for i in range(4)], axis=1
                )
                for e in range(2)
            ],
            axis=0,
        )
        out_part[k * CH : (k + 1) * CH, :] = jnp.dot(
            attended, w_all[...], preferred_element_type=f32
        ).astype(bf16)

        for n, e in enumerate(far_first(y, c)):
            block = k * 8 + lax.rem(e, 2) * 4 + e // 2
            device = ((e // 2) * 4 + k * 2 + lax.rem(e, 2), 4 * x + own)
            send = copy(OUT_RS, out_part.at[part(block, B)], r_out.at[out_slot], device)
            if n < 7:
                send.start()
            else:
                pl.when((zh != k) | jnp.logical_not(out_self))(send.start)

    rows(EMB_RS, pick, 15 * B).wait_send()
    rows(EMB_AG + mine_k, x_all, 15 * B).wait_send()
    rows(K_MOVE, keys, 3 * F).wait_send()
    rows(V_MOVE, values, 3 * F).wait_send()
    rows(W_MOVE, w_stage, 3 * HD).wait_send()
    rows(K_PAIR, keys, PROMPT // 2).wait_send()
    rows(V_PAIR, values, PROMPT // 2).wait_send()
    for k in range(2):
        rows(Q_RS + k, q_part, 7 * Q).wait_send()
        rows(Q_Z + k, q_mine, Q).wait_send()
        rows(O_Z + k, o_mine, Q + B).wait_send()
        rows(ATT_AG + k, att_all, 7 * Q).wait_send()
    rows(KV_PAIR, kv_part, 8 * HALF).wait_send()
    rows(KV_RS, kv_far, 6 * HALF).wait_send()
    rows(KV_Z, kv_mine, 2 * HALF).wait_send()
    rows(W_TURN, w_stage, 3 * HD).wait_send()


    @pl.when(out_self)
    def _():
        r_out[out_slot, :] = out_part[part(zh * 8 + c * 4 + y, B), :]
        rows(OUT_RS, r_out, 15 * B).wait_recv()

    @pl.when(jnp.logical_not(out_self))
    def _():
        rows(OUT_RS, r_out, 16 * B).wait_recv()

    out_ref[...] = slot_sum(r_out, N, B).astype(bf16)

    @pl.when(out_self)
    def _():
        rows(OUT_RS, out_part, 15 * B).wait_send()

    @pl.when(jnp.logical_not(out_self))
    def _():
        rows(OUT_RS, out_part, 16 * B).wait_send()


def rotation_table(first, count):
    half = HD // 2
    frequency = 10000.0 ** (-np.arange(half, dtype=np.float64) / half)
    angles = (first + np.arange(count, dtype=np.float64))[:, None] * frequency[None, :]
    cosine, sine = np.cos(angles), np.sin(angles)
    return np.concatenate(
        [np.concatenate([cosine, cosine], 1), np.concatenate([-sine, sine], 1)], 0
    ).astype(np.float32)


def body(gen_ids, embed_rows, w_query, w_key, w_value, w_out, prompt_keys, prompt_values):
    table = jnp.asarray(rotation_table(prompt_keys.shape[0] * N, B))

    def held(count, width=HD, dtype=bf16):
        return pltpu.VMEM((count, width), dtype)

    return pl.pallas_call(
        kernel,
        out_shape=jax.ShapeDtypeStruct((B, F), bf16),
        in_specs=[pl.BlockSpec(memory_space=pl.ANY)] * 9,
        out_specs=pl.BlockSpec(memory_space=pltpu.VMEM),
        scratch_shapes=[
            held(N, B, jnp.int32), held(F, F), held(F, F), held(F, F), held(F, F), held(2 * B, HD, f32),
            held(PROMPT), held(PROMPT), held(F, F), held(F, F),
            held(N * B, F), held(N * B, F), held(N * B, F),
            held(8 * HALF), held(8 * HALF), held(HALF), held(HALF),
            held(16 * HALF), held(8 * HALF), held(8 * HALF), held(2 * HALF), held(2 * HALF),
            held(HALF, PROMPT, f32), held(HALF + 2 * B), held(HALF + 2 * B),
            held(HALF), held(8 * HALF), held(N * B, F), held(N * B, F),
            pltpu.SemaphoreType.DMA((9,)),
            pltpu.SemaphoreType.DMA((21,)),
            pltpu.SemaphoreType.DMA((21,)),
        ],
        compiler_params=pltpu.CompilerParams(
            collective_id=0, has_side_effects=True, vmem_limit_bytes=62 * 1024 * 1024
        ),
    )(gen_ids, embed_rows, w_query, w_key, w_value, w_out, prompt_keys, prompt_values, table)


def solution(mesh):
    return jax.shard_map(
        body,
        mesh=mesh,
        in_specs=(
            P(), P("head", "seq"), P("seq", "head"), P("seq", "head"), P("seq", "head"),
            P("head", "seq"), P("seq", "head"), P("seq", "head"),
        ),
        out_specs=P("seq", "head"),
        check_vma=False,
    )
```
